128 devices in a mesh: snap: 4 (over y), vert: 32 (over z, x, core).
Axes of the slice: x: 4, y: 4, z: 4, core: 2. Of those that a mesh axis runs over, the one named last changes fastest.
Arguments:
- features: bfloat16 [32, 8192, 256], P('snap', 'vert'), may hold values from -6 to 6
- tile_cols: int32 [32, 64, 4], P('snap', 'vert'), may hold values from -1 to 63, as said below
- counts: int32 [32, 64], P('snap', 'vert'), may hold values from 1 to 4
- birth_snap: int32 [8192], P('vert'), may hold values from 0 to 31
- query_proj: bfloat16 [256, 256], replicated, may hold values from -0.375 to 0.375
- keyval_proj: bfloat16 [256, 512], replicated, may hold values from -0.375 to 0.375
- struct_out: bfloat16 [256, 256], replicated, may hold values from -0.375 to 0.375
- position_embedding_table: bfloat16 [32, 256], replicated, may hold values from -3 to 3
- temporal_qkv_weight: bfloat16 [256, 768], replicated, may hold values from -0.375 to 0.375
- temporal_output_weight: bfloat16 [256, 256], replicated, may hold values from -0.375 to 0.375
Outputs:
- embeddings: float32 [32, 32, 4, 64, 256], P(None, 'vert', 'snap')
The draws below stay inside these ranges and needn't reach their ends.
Inputs may be any that keep to these rules, and one draw needn't show every extreme that they name: `tile_cols`: entries k < counts[s, r] name column blocks of occupied tiles (a block may appear twice); the others are -1. Of the live entries of the 8 x 2 row blocks of one device, at most 3 lie in column blocks of any one index of vert, and exactly 3 for one index.
All inputs are finite; a program needn't handle non-finite values.
Results may differ from the reference program's by a relative error of at most 0.008.
Values may be sent and summed in bfloat16 or wider, within the bound.
A program may use at most 128 MiB of HBM per device.

```python
import jax
import jax.numpy as jnp
from jax import lax

D = 256
HEADS = 8
TILE = 128
KT = 4
SNAP_DEV = 8
BLK_DEV = 2
S = 32
NB = 64
V = 8192
VQ = 64
N_SNAP = 4
N_VERT = 32


def tile_table(key):
    key = jax.random.fold_in(key, 7)
    key_counts, key_rest = jax.random.split(key)
    count_table = jax.random.randint(key_counts, (S, NB), 1, KT + 1).astype(jnp.int32)
    flat = SNAP_DEV * BLK_DEV * KT
    capacity = max(2, (flat + N_VERT - 2) // (N_VERT - 1))
    devices = N_SNAP * N_VERT
    per_device = count_table.reshape(N_SNAP, SNAP_DEV, N_VERT, BLK_DEV).transpose(0, 2, 1, 3).reshape(devices, SNAP_DEV * BLK_DEV)
    live = (jnp.arange(KT, dtype=jnp.int32)[None, None, :] < per_device[:, :, None]).reshape(devices, flat)
    device_keys = jax.random.split(key_rest, devices)

    def one_device(live_row, device_key):
        key_perm, key_hot, key_remainder, key_within = jax.random.split(device_key, 4)
        shuffle = jax.random.permutation(key_perm, flat).astype(jnp.int32)
        ranking = jnp.where(live_row, 0, flat).astype(jnp.int32) + shuffle
        ordering = jnp.argsort(ranking, stable=True).astype(jnp.int32)
        position = jnp.argsort(ordering, stable=True).astype(jnp.int32)
        busiest_tile = jax.random.randint(key_hot, (), 0, N_VERT).astype(jnp.int32)
        others = jax.random.permutation(key_remainder, N_VERT - 1).astype(jnp.int32)
        others = others + (others >= busiest_tile).astype(jnp.int32)
        owning_devices = jnp.where(position < capacity, busiest_tile, others[(position - capacity) % (N_VERT - 1)])
        within = jax.random.randint(key_within, (flat,), 0, BLK_DEV).astype(jnp.int32)
        return jnp.where(live_row, owning_devices * BLK_DEV + within, -1).astype(jnp.int32)
    columns = jax.vmap(one_device)(live, device_keys)
    columns = columns.reshape(N_SNAP, N_VERT, SNAP_DEV, BLK_DEV, KT).transpose(0, 2, 1, 3, 4).reshape(S, NB, KT)
    return (columns, count_table)


def draw_tile_cols(key, part):
    return tile_table(key)[0]


def draw_counts(key, part):
    return tile_table(key)[1]


def draw_features(key, part):
    key_base = jax.random.fold_in(key, 0)
    values = jax.random.truncated_normal(key_base, -6.0, 6.0, (S, V, D), jnp.float32)
    return values.astype(jnp.bfloat16)


def plant(drawn, stream_key, least, largest):
    spot = [jax.random.randint(jax.random.fold_in(stream_key, axis), (), 0, length) for axis, length in enumerate(drawn.shape)]
    widest = drawn.shape.index(max(drawn.shape))
    next_to = spot[:widest] + [(spot[widest] + 1) % drawn.shape[widest]] + spot[widest + 1:]
    return drawn.at[tuple(spot)].set(least).at[tuple(next_to)].set(largest)


def gaussian(key, extent, scale, bound, held_as=jnp.bfloat16):
    values = scale * jax.random.normal(key, extent, jnp.float32)
    return jnp.clip(values, min=-bound, max=bound).astype(held_as)


def setup_inputs(seed: int = 0) -> dict:
    keys = jax.random.split(jax.random.key(seed), 11)
    features = draw_features(jax.random.fold_in(keys[10], 71), 0)
    tile_cols = draw_tile_cols(jax.random.fold_in(keys[10], 71), 0)
    counts = draw_counts(jax.random.fold_in(keys[10], 71), 0)
    birth_snap = plant(jax.random.randint(keys[3], (V,), 0, S), jax.random.fold_in(keys[3], 1), 0, S - 1).astype(jnp.int32)
    query_proj = gaussian(keys[4], (D, D), D ** -0.5, 0.375)
    keyval_proj = gaussian(keys[5], (D, 2 * D), D ** -0.5, 0.375)
    struct_out = gaussian(keys[6], (D, D), D ** -0.5, 0.375)
    position_embedding_table = gaussian(keys[7], (S, D), 0.5, 3.0)
    temporal_qkv_weight = gaussian(keys[8], (D, 3 * D), D ** -0.5, 0.375)
    temporal_output_weight = gaussian(keys[9], (D, D), D ** -0.5, 0.375)
    return {"features": features, "tile_cols": tile_cols, "counts": counts, "birth_snap": birth_snap, "query_proj": query_proj, "keyval_proj": keyval_proj, "struct_out": struct_out, "position_embedding_table": position_embedding_table, "temporal_qkv_weight": temporal_qkv_weight, "temporal_output_weight": temporal_output_weight}


def attend_tiles(query_rows_all, key_rows, live_keys):
    count, span, model_width = query_rows_all.shape
    head_size = model_width // HEADS
    length = key_rows.shape[1]
    heads_q = query_rows_all.reshape(count, span, HEADS, head_size).astype(jnp.float32)
    keys_h = key_rows[:, :, :model_width].reshape(count, length, HEADS, head_size).astype(jnp.float32)
    values_h = key_rows[:, :, model_width:].reshape(count, length, HEADS, head_size).astype(jnp.float32)
    scores = jnp.einsum("bqhe,bkhe->bhqk", heads_q, keys_h) * (head_size ** -0.5)
    scores = jnp.where(live_keys[:, None, None, :], scores, -jnp.inf)
    weight_matrices = jax.nn.softmax(scores, axis=-1).astype(jnp.bfloat16)
    blended_rows = jnp.einsum("bhqk,bkhe->bqhe", weight_matrices.astype(jnp.float32), values_h)
    return blended_rows.astype(jnp.bfloat16).reshape(count, span, model_width)


def time_layer(hidden_block, births, position_embedding_table, temporal_qkv_weight, temporal_output_weight):
    length, count, model_width = hidden_block.shape
    head_size = model_width // HEADS
    blended_input = (hidden_block.astype(jnp.float32) + position_embedding_table.astype(jnp.float32)[:, None, :]).astype(jnp.bfloat16)
    projected_rows = jnp.einsum("mcf,fz->mcz", blended_input.astype(jnp.float32), temporal_qkv_weight.astype(jnp.float32)).astype(jnp.bfloat16)
    query_rows_all = projected_rows[:, :, :model_width].reshape(length, count, HEADS, head_size).astype(jnp.float32)
    keys_h = projected_rows[:, :, model_width:2 * model_width].reshape(length, count, HEADS, head_size).astype(jnp.float32)
    values_h = projected_rows[:, :, 2 * model_width:].reshape(length, count, HEADS, head_size).astype(jnp.float32)
    scores = jnp.einsum("snhe,tnhe->nhst", query_rows_all, keys_h) * (head_size ** -0.5)
    later = jnp.arange(length, dtype=jnp.int32)[:, None]
    earlier = jnp.arange(length, dtype=jnp.int32)[None, :]
    allowed = ((earlier <= later)[None] & (earlier[None] >= births[:, None, None])) | (earlier == later)[None]
    scores = jnp.where(allowed[:, None], scores, -jnp.inf)
    weight_matrices = jax.nn.softmax(scores, axis=-1).astype(jnp.bfloat16)
    blended_rows = jnp.einsum("nhst,tnhe->snhe", weight_matrices.astype(jnp.float32), values_h)
    blended_rows = blended_rows.astype(jnp.bfloat16).reshape(length, count, model_width)
    update_rows = jnp.einsum("mcf,fz->mcz", blended_rows.astype(jnp.float32), temporal_output_weight.astype(jnp.float32))
    return hidden_block.astype(jnp.float32) + update_rows


def reference(features, tile_cols, counts, birth_snap, query_proj, keyval_proj, struct_out, position_embedding_table, temporal_qkv_weight, temporal_output_weight):
    def snapshot(pieces):
        frame, cols, count_row = pieces
        query_rows_all = jnp.dot(frame, query_proj, preferred_element_type=jnp.float32).astype(jnp.bfloat16).reshape(NB, TILE, D)
        keyval = jnp.dot(frame, keyval_proj, preferred_element_type=jnp.float32).astype(jnp.bfloat16).reshape(NB, TILE, 2 * D)
        live_tiles = jnp.arange(KT, dtype=jnp.int32)[None, :] < count_row[:, None]
        index = jnp.where(live_tiles, cols, 0).astype(jnp.int32)
        key_rows = keyval[index].reshape(NB, KT * TILE, 2 * D)
        live_keys = jnp.repeat(live_tiles, TILE, axis=1)
        attended = attend_tiles(query_rows_all, key_rows, live_keys).reshape(V, D)
        update_rows = jnp.dot(attended, struct_out, preferred_element_type=jnp.float32)
        return (frame.astype(jnp.float32) + update_rows).astype(jnp.bfloat16)

    hidden = lax.map(snapshot, (features, tile_cols, counts))
    grouped = hidden.reshape(S, NB, TILE, D).transpose(1, 0, 2, 3)
    born = birth_snap.reshape(NB, TILE)

    def vertex_block(pieces):
        block, births = pieces
        return time_layer(block, births, position_embedding_table, temporal_qkv_weight, temporal_output_weight)

    result = lax.map(vertex_block, (grouped, born))
    result = result.transpose(1, 0, 2, 3).reshape(S, V, D)
    return result.reshape(S, N_VERT, N_SNAP, VQ, D)
```

```python
import functools

import jax
import jax.numpy as jnp
from jax import lax
from jax.experimental import pallas as pl
from jax.experimental.pallas import tpu as pltpu
from jax.sharding import PartitionSpec as P

HEADS = 8
TILE = 128
D = 256
HS = D // HEADS
KT = 4
BLOCKS = 16
RING = 4
RANKS = 3
SLOTS = 2 * RING * RING * RANKS
SCALE = 1.4426950408889634 * HS**-0.5
MESH = pl.DeviceIdType.MESH
NT = (((1,), (1,)), ((), ()))
TN = (((0,), (0,)), ((), ()))
NN = (((1,), (0,)), ((), ()))
ORDER = (0, 1, 3, 2)


def dot(a, b, dims=NN):
    return lax.dot_general(a, b, dims, preferred_element_type=jnp.float32)


def vert_id(z, x, core):
    return (z * RING + x) * 2 + core


def position():
    v = lax.axis_index("vert")
    return v // (2 * RING), (v // 2) % RING, v % 2


def prep_kernel(cols, counts, req, blk, table, used):
    z, x, core = position()

    @pl.loop(0, SLOTS)
    def _(n):
        blk[n] = 0

    @pl.loop(0, 8)
    def _(row):
        for n in range(RING * RANKS):
            req[row, n] = 0
        for n in range(RING):
            used[row, n] = 0

    @pl.loop(0, BLOCKS)
    def _(b):
        live = counts[b]
        for k in range(KT):
            col = cols[b, k]
            alive = k < live
            owner = jnp.where(alive, col // 2, 0)
            oz, ox, oc = owner // (2 * RING), (owner // 2) % RING, owner % 2
            dz, dx = (oz - z + RING) % RING, (x - ox + RING) % RING
            ez, ex = (z - oz + RING) % RING, (ox - x + RING) % RING
            i = jnp.where(oc == 0, dx, ez)
            j = jnp.where(oc == 0, dz, ex)
            row = jnp.where(oc == core, 0, RING) + i
            rank = used[row, j]
            place = (row * RING + j) * RANKS + rank

            @pl.when(alive)
            def _():
                used[row, j] = rank + 1
                req[row, j * RANKS + rank] = (b // 2) * 2 + col % 2
                blk[place] = b

            table[b, k] = jnp.where(alive, place, -1)


def fetch_kernel(
    req, blk, table, wire, feat, wq_in, wkv_in, wso, arr,
    codes_v, codes, ag1, ag2, ag3, stage, recv, wq, wt, part, top, total, hid,
    req_send, req_recv, loc_sem, ag_send, ag_recv, tile_send, tile_recv, snap_send, snap_recv, own_sem,
):
    z, x, core = position()
    y = lax.axis_index("snap")
    flat = core == 0

    def gather_peer(j):
        return vert_id(
            jnp.where(flat, (z + j) % RING, z), jnp.where(flat, x, (x + j) % RING), core
        )

    def dest(row):
        i = row % RING
        other = row // RING
        return vert_id(
            jnp.where(flat, z, (z + i) % RING),
            jnp.where(flat, (x + i) % RING, x),
            (core + other) % 2,
        )

    def relay(row):
        i = row % RING
        c = (core + row // RING) % 2
        return vert_id(
            jnp.where(c == 0, z, (z + RING - i) % RING),
            jnp.where(c == 0, (x + RING - i) % RING, x),
            c,
        )

    barrier = pltpu.get_barrier_semaphore()
    greet = [gather_peer(1), gather_peer(2), gather_peer(3)]
    greet += [dest(r) for r in range(1, 8)]
    greet += [relay(r) for r in range(5, 8)]
    for v in greet:
        pl.semaphore_signal(barrier, inc=1, device_id=(y, v), device_id_type=MESH)
    for i in range(1, RING):
        pl.semaphore_signal(
            barrier, inc=1, device_id=((y + i) % RING, lax.axis_index("vert")), device_id_type=MESH
        )
    pl.semaphore_wait(barrier, len(greet) + RING - 1)

    def ask(row):
        return pltpu.make_async_remote_copy(
            src_ref=wire.at[row],
            dst_ref=codes_v.at[row],
            send_sem=req_send.at[row],
            recv_sem=req_recv.at[row],
            device_id=(y, relay(row)),
            device_id_type=MESH,
        )

    for row in range(1, 8):
        ask(row).start()

    gathered = {1: ag1, 2: ag2, 3: ag3}

    def share(j):
        return pltpu.make_async_remote_copy(
            src_ref=feat,
            dst_ref=gathered[j],
            send_sem=ag_send.at[j - 1],
            recv_sem=ag_recv.at[j - 1],
            device_id=(y, gather_peer(RING - j)),
            device_id_type=MESH,
        )

    for j in ORDER[1:]:
        share(j).start()

    wt[0] = wq_in[...].astype(jnp.float32).T.astype(jnp.bfloat16)
    wt[1] = wkv_in[:, D:].astype(jnp.float32).T.astype(jnp.bfloat16)

    @pl.loop(0, BLOCKS)
    def _(b):
        q = (dot(wt[0], feat[b], NT) * SCALE).astype(jnp.bfloat16)
        zero = jnp.zeros((HS, TILE), jnp.bfloat16)
        for h in range(HEADS):
            p, lo = h // 2, (h % 2) * TILE
            base = (h % 4) * HS
            for g in range(4):
                if g != h % 4:
                    wq[b, p, g * HS : (g + 1) * HS, lo : lo + TILE] = zero
            wq[b, p, base : base + HS, lo : lo + TILE] = q[h * HS : (h + 1) * HS]

    for row in range(1, 8):
        ask(row).wait()
    down = pltpu.make_async_copy(codes_v.at[pl.ds(1, 7)], codes.at[pl.ds(1, 7)], loc_sem)
    down.start()
    down.wait()

    def send(row, j):
        return pltpu.make_async_remote_copy(
            src_ref=stage.at[row, j],
            dst_ref=recv.at[row, j],
            send_sem=tile_send.at[row, j],
            recv_sem=tile_recv.at[row, j],
            device_id=(y, dest(row)),
            device_id_type=MESH,
        )

    for j in ORDER:
        if j:
            share(j).wait_recv()
        source = gathered[j] if j else feat

        @pl.loop(1, 8)
        def _(row):
            for r in range(RANKS):
                stage[row, j, r] = source[codes[row, 0, j * RANKS + r]]
            send(row, j).start()

        for r in range(RANKS):
            recv[0, j, r] = source[req[0, j * RANKS + r]]

    def attend(row, j, r):
        n = (row * RING + j) * RANKS + r
        b = blk[n]
        rows = recv[row, j, r]
        keys = dot(rows, wkv_in[:, :D]).astype(jnp.bfloat16)
        values = dot(wt[1], rows, NT).astype(jnp.bfloat16)
        for p in range(HEADS // 2):
            half = (p // 2) * TILE
            s = dot(keys[:, half : half + TILE], wq[b, p])
            m = jnp.max(s, axis=0, keepdims=True)
            e = jnp.exp2(s - m)
            t = jnp.sum(e, axis=0, keepdims=True)
            o = dot(values[2 * p * HS : 2 * (p + 1) * HS], e.astype(jnp.bfloat16))
            for g in range(2):
                h = 2 * p + g
                top[n, h : h + 1] = m[:, g * TILE : (g + 1) * TILE]
                total[n, h : h + 1] = t[:, g * TILE : (g + 1) * TILE]
                part[n, h * HS : (h + 1) * HS] = o[g * HS : (g + 1) * HS, g * TILE : (g + 1) * TILE]

    for j in ORDER:
        for r in range(RANKS):
            attend(0, j, r)

        @pl.loop(1, 8)
        def _(row):
            send(row, j).wait_recv()

            @pl.loop(0, RANKS)
            def _(r):
                attend(row, j, r)

    def spread(i, half):
        group = (y + i) % RING
        return pltpu.make_async_remote_copy(
            src_ref=hid.at[pl.ds(half * 4, 4), pl.ds(group * 64, 64)],
            dst_ref=arr.at[pl.ds(y * 8 + half * 4, 4)],
            send_sem=snap_send.at[half, i],
            recv_sem=snap_recv.at[half, i],
            device_id=(group, lax.axis_index("vert")),
            device_id_type=MESH,
        )

    for half in range(2):

        @pl.loop(half * 4, half * 4 + 4)
        def _(s):
            for u in range(2):
                b = s * 2 + u
                slots, live, tops = [], [], []
                for k in range(KT):
                    slot = table[b, k]
                    alive = slot >= 0
                    slot = jnp.where(alive, slot, 0)
                    slots.append(slot)
                    live.append(jnp.where(alive, jnp.float32(0), jnp.float32(-jnp.inf)))
                    tops.append(top[slot] + live[k])
                m = functools.reduce(jnp.maximum, tops)
                weights = [jnp.exp2(t - m) for t in tops]
                denominator = sum(weights[k] * total[slots[k]] for k in range(KT))
                weights = [w / denominator for w in weights]
                parts = []
                for h in range(HEADS):
                    parts.append(
                        sum(
                            weights[k][h : h + 1] * part[slots[k], h * HS : (h + 1) * HS]
                            for k in range(KT)
                        )
                    )
                attended = jnp.concatenate(parts, axis=0).T.astype(jnp.bfloat16)
                update = dot(attended, wso[...])
                hid[s, u * TILE : (u + 1) * TILE] = (feat[b].astype(jnp.float32) + update).astype(
                    jnp.bfloat16
                )

        for i in (2, 1, 3):
            spread(i, half).start()

    own = pltpu.make_async_copy(hid.at[:, pl.ds(y * 64, 64)], arr.at[pl.ds(y * 8, 8)], own_sem)
    own.start()
    own.wait()
    for half in range(2):
        for i in range(1, RING):
            spread(i, half).wait()
    for j in ORDER:
        if j:
            share(j).wait_send()

        @pl.loop(1, 8)
        def _(row):
            send(row, j).wait_send()


def time_kernel(births, arr, pos, wqkv, wo, out, wt):
    y = lax.axis_index("snap")
    step = pl.program_id(0)

    @pl.when(step == 0)
    def _():
        wt[0] = wqkv[:, :D].astype(jnp.float32).T.astype(jnp.bfloat16)
        wt[1] = wqkv[:, 2 * D :].astype(jnp.float32).T.astype(jnp.bfloat16)

    snaps = pos.shape[0]
    n = snaps * 8
    hidden = arr[...].astype(jnp.float32)
    positions = pos[...].astype(jnp.float32)[:, None, :]
    lane_head = lax.broadcasted_iota(jnp.int32, (1, TILE), 1) // HS
    vertex = lax.broadcasted_iota(jnp.int32, (1, 8, 1), 1)
    lane = lax.broadcasted_iota(jnp.int32, (1, 1, n), 2)
    key_snap = lax.broadcasted_iota(jnp.int32, (snaps, 1, 1), 0)
    for g in range(2):
        base = y * 64 + step * 16 + g * 8
        birth = jnp.zeros((1, 8, 1), jnp.int32)
        for v in range(8):
            birth = jnp.where(vertex == v, births[base + v], birth)
        query_snap = lane // 8
        allowed = (lane % 8 == vertex) & (
            (query_snap == key_snap) | ((query_snap >= key_snap) & (key_snap >= birth))
        )
        bias = jnp.where(allowed, jnp.float32(0), jnp.float32(-jnp.inf)).reshape(n, n)
        mine = hidden[:, g * 8 : (g + 1) * 8]
        rows = (mine + positions).reshape(n, D).astype(jnp.bfloat16)
        q = (dot(wt[0], rows, NT) * SCALE).astype(jnp.bfloat16)
        keys = dot(rows, wqkv[:, D : 2 * D]).astype(jnp.bfloat16)
        values = dot(wt[1], rows, NT).astype(jnp.bfloat16)
        mixed = []
        for h in range(HEADS):
            half = (h // 4) * TILE
            mask = (lane_head == h % 4).astype(jnp.float32).astype(jnp.bfloat16)
            s = dot(keys[:, half : half + TILE] * mask, q[half : half + TILE]) + bias
            m = jnp.max(s, axis=0, keepdims=True)
            e = jnp.exp2(s - m)
            t = jnp.sum(e, axis=0, keepdims=True)
            o = dot(values[h * HS : (h + 1) * HS], e.astype(jnp.bfloat16))
            mixed.append(o / t)
        mixed = jnp.concatenate(mixed, axis=0).T.astype(jnp.bfloat16)
        out[:, g * 8 : (g + 1) * 8] = mine + dot(mixed, wo[...]).reshape(snaps, 8, D)


def local(features, tile_cols, counts, births, wq, wkv, wso, pos, wqkv, wo):
    snaps, rows, width = features.shape
    smem = pl.BlockSpec(memory_space=pltpu.SMEM)
    vmem = pl.BlockSpec(memory_space=pltpu.VMEM)
    hbm = pl.BlockSpec(memory_space=pl.ANY)
    dma = pltpu.SemaphoreType.DMA
    req, blk, table = pl.pallas_call(
        prep_kernel,
        out_shape=(
            jax.ShapeDtypeStruct((8, 128), jnp.int32),
            jax.ShapeDtypeStruct((SLOTS,), jnp.int32),
            jax.ShapeDtypeStruct((BLOCKS, KT), jnp.int32),
        ),
        in_specs=[smem] * 2,
        out_specs=(smem,) * 3,
        scratch_shapes=[pltpu.SMEM((8, RING), jnp.int32)],
        name="rank_entries",
    )(tile_cols.reshape(BLOCKS, KT), counts.reshape(BLOCKS))
    half = jnp.bfloat16
    arrived = pl.pallas_call(
        fetch_kernel,
        out_shape=jax.ShapeDtypeStruct((RING * snaps, rows // RING, width), half),
        in_specs=[smem] * 3 + [vmem] * 5,
        out_specs=hbm,
        scratch_shapes=[
            pltpu.VMEM((8, 1, 128), jnp.int32),
            pltpu.SMEM((8, 1, 128), jnp.int32),
            pltpu.VMEM((BLOCKS, TILE, width), half),
            pltpu.VMEM((BLOCKS, TILE, width), half),
            pltpu.VMEM((BLOCKS, TILE, width), half),
            pltpu.VMEM((8, RING, RANKS, TILE, width), half),
            pltpu.VMEM((8, RING, RANKS, TILE, width), half),
            pltpu.VMEM((BLOCKS, HEADS // 2, TILE, 2 * TILE), half),
            pltpu.VMEM((2, width, width), half),
            pltpu.VMEM((SLOTS, width, TILE), jnp.float32),
            pltpu.VMEM((SLOTS, HEADS, TILE), jnp.float32),
            pltpu.VMEM((SLOTS, HEADS, TILE), jnp.float32),
            pltpu.VMEM((snaps, rows, width), half),
            dma((8,)), dma((8,)), dma, dma((3,)), dma((3,)),
            dma((8, RING)), dma((8, RING)), dma((2, RING)), dma((2, RING)), dma,
        ],
        compiler_params=pltpu.CompilerParams(
            collective_id=0, has_side_effects=True, vmem_limit_bytes=56 * 2**20
        ),
        name="fetch_attend",
    )(req, blk, table, req.reshape(8, 1, 128), features.reshape(BLOCKS, TILE, width), wq, wkv, wso)
    count = rows // RING
    result = pl.pallas_call(
        time_kernel,
        out_shape=jax.ShapeDtypeStruct((RING * snaps, count, width), jnp.float32),
        grid=(count // 16,),
        in_specs=[
            smem,
            pl.BlockSpec((RING * snaps, 16, width), lambda i: (0, i, 0)),
            pl.BlockSpec(pos.shape, lambda i: (0, 0)),
            pl.BlockSpec(wqkv.shape, lambda i: (0, 0)),
            pl.BlockSpec(wo.shape, lambda i: (0, 0)),
        ],
        out_specs=pl.BlockSpec((RING * snaps, 16, width), lambda i: (0, i, 0)),
        scratch_shapes=[pltpu.VMEM((2, width, width), half)],
        compiler_params=pltpu.CompilerParams(vmem_limit_bytes=48 * 2**20),
        name="attend_time",
    )(births, arrived, pos, wqkv, wo)
    return result[:, None, None]


def solution(mesh):
    placed = (
        P("snap", "vert", None), P("snap", "vert", None), P("snap", "vert"), P("vert"),
        P(), P(), P(), P(), P(), P(),
    )
    return jax.shard_map(
        local,
        mesh=mesh,
        in_specs=placed,
        out_specs=P(None, "vert", "snap", None, None),
        check_vma=False,
    )
```

```python
import functools

import jax
import jax.numpy as jnp
from jax import lax
from jax.experimental import pallas as pl
from jax.experimental.pallas import tpu as pltpu
from jax.sharding import PartitionSpec as P

HEADS = 8
TILE = 128
D = 256
HS = D // HEADS
KT = 4
BLOCKS = 16
RING = 4
RANKS = 3
SLOTS = 2 * RING * RING * RANKS
SCALE = 1.4426950408889634 * HS**-0.5
MESH = pl.DeviceIdType.MESH
NT = (((1,), (1,)), ((), ()))
TN = (((0,), (0,)), ((), ()))
NN = (((1,), (0,)), ((), ()))
ORDER = (0, 1, 3, 2)


def dot(a, b, dims=NN):
    return lax.dot_general(a, b, dims, preferred_element_type=jnp.float32)


def vert_id(z, x, core):
    return (z * RING + x) * 2 + core


def position():
    v = lax.axis_index("vert")
    return v // (2 * RING), (v // 2) % RING, v % 2


def prep_kernel(cols, counts, req, blk, table, used):
    z, x, core = position()

    @pl.loop(0, SLOTS)
    def _(n):
        blk[n] = 0

    @pl.loop(0, 8)
    def _(row):
        for n in range(RING * RANKS):
            req[row, n] = 0
        for n in range(RING):
            used[row, n] = 0

    @pl.loop(0, BLOCKS)
    def _(b):
        live = counts[b]
        for k in range(KT):
            col = cols[b, k]
            alive = k < live
            owner = jnp.where(alive, col // 2, 0)
            oz, ox, oc = owner // (2 * RING), (owner // 2) % RING, owner % 2
            dz, dx = (oz - z + RING) % RING, (x - ox + RING) % RING
            ez, ex = (z - oz + RING) % RING, (ox - x + RING) % RING
            i = jnp.where(oc == 0, dx, ez)
            j = jnp.where(oc == 0, dz, ex)
            row = jnp.where(oc == core, 0, RING) + i
            rank = used[row, j]
            place = (row * RING + j) * RANKS + rank

            @pl.when(alive)
            def _():
                used[row, j] = rank + 1
                req[row, j * RANKS + rank] = (b // 2) * 2 + col % 2
                blk[place] = b

            table[b, k] = jnp.where(alive, place, -1)


def fetch_kernel(
    req, blk, table, wire, feat, wq_in, wkv_in, wso, arr,
    codes_v, codes, ag1, ag2, ag3, stage, recv, wq, wt, part, top, total, hid,
    req_send, req_recv, loc_sem, ag_send, ag_recv, tile_send, tile_recv, snap_send, snap_recv, own_sem,
):
    z, x, core = position()
    y = lax.axis_index("snap")
    flat = core == 0

    def gather_peer(j):
        return vert_id(
            jnp.where(flat, (z + j) % RING, z), jnp.where(flat, x, (x + j) % RING), core
        )

    def dest(row):
        i = row % RING
        other = row // RING
        return vert_id(
            jnp.where(flat, z, (z + i) % RING),
            jnp.where(flat, (x + i) % RING, x),
            (core + other) % 2,
        )

    def relay(row):
        i = row % RING
        c = (core + row // RING) % 2
        return vert_id(
            jnp.where(c == 0, z, (z + RING - i) % RING),
            jnp.where(c == 0, (x + RING - i) % RING, x),
            c,
        )

    barrier = pltpu.get_barrier_semaphore()
    greet = [gather_peer(1), gather_peer(2), gather_peer(3)]
    greet += [dest(r) for r in range(1, 8)]
    greet += [relay(r) for r in range(5, 8)]
    for v in greet:
        pl.semaphore_signal(barrier, inc=1, device_id=(y, v), device_id_type=MESH)
    for i in range(1, RING):
        pl.semaphore_signal(
            barrier, inc=1, device_id=((y + i) % RING, lax.axis_index("vert")), device_id_type=MESH
        )
    pl.semaphore_wait(barrier, len(greet) + RING - 1)

    def ask(row):
        return pltpu.make_async_remote_copy(
            src_ref=wire.at[row],
            dst_ref=codes_v.at[row],
            send_sem=req_send.at[row],
            recv_sem=req_recv.at[row],
            device_id=(y, relay(row)),
            device_id_type=MESH,
        )

    for row in range(1, 8):
        ask(row).start()

    gathered = {1: ag1, 2: ag2, 3: ag3}

    def share(j):
        return pltpu.make_async_remote_copy(
            src_ref=feat,
            dst_ref=gathered[j],
            send_sem=ag_send.at[j - 1],
            recv_sem=ag_recv.at[j - 1],
            device_id=(y, gather_peer(RING - j)),
            device_id_type=MESH,
        )

    for j in ORDER[1:]:
        share(j).start()

    wt[0] = wq_in[...].astype(jnp.float32).T.astype(jnp.bfloat16)
    wt[1] = wkv_in[:, D:].astype(jnp.float32).T.astype(jnp.bfloat16)

    @pl.loop(0, BLOCKS)
    def _(b):
        q = (dot(wt[0], feat[b], NT) * SCALE).astype(jnp.bfloat16)
        wq[b, 0] = q[:TILE]
        wq[b, 1] = q[TILE:]

    for row in range(1, 8):
        ask(row).wait()
    down = pltpu.make_async_copy(codes_v.at[pl.ds(1, 7)], codes.at[pl.ds(1, 7)], loc_sem)
    down.start()
    down.wait()

    def send(row, j):
        return pltpu.make_async_remote_copy(
            src_ref=stage.at[row, j],
            dst_ref=recv.at[row, j],
            send_sem=tile_send.at[row, j],
            recv_sem=tile_recv.at[row, j],
            device_id=(y, dest(row)),
            device_id_type=MESH,
        )

    for j in ORDER:
        if j:
            share(j).wait_recv()
        source = gathered[j] if j else feat

        @pl.loop(1, 8)
        def _(row):
            for r in range(RANKS):
                stage[row, j, r] = source[codes[row, 0, j * RANKS + r]]
            send(row, j).start()

        for r in range(RANKS):
            recv[0, j, r] = source[req[0, j * RANKS + r]]

    lane_head = lax.broadcasted_iota(jnp.int32, (1, TILE), 1) // HS
    masks = [(lane_head == g).astype(jnp.float32).astype(jnp.bfloat16) for g in range(4)]

    def attend3(row, j):
        rows3 = recv[row, j].reshape(RANKS * TILE, D)
        keys3 = dot(rows3, wkv_in[:, :D]).astype(jnp.bfloat16)
        values3 = dot(wt[1], rows3, NT).astype(jnp.bfloat16)
        for r in range(RANKS):
            attend(row, j, r, keys3[r * TILE : (r + 1) * TILE], values3[:, r * TILE : (r + 1) * TILE])

    def attend(row, j, r, keys, values):
        n = (row * RING + j) * RANKS + r
        b = blk[n]

        for half in range(2):
            kh = keys[:, half * TILE : (half + 1) * TILE]
            s = dot(jnp.concatenate([kh * w for w in masks], axis=0), wq[b, half])
            s = s.reshape(4, TILE, TILE)
            m = jnp.max(s, axis=1)
            e = jnp.exp2(s - m[:, None])
            top[n, half * 4 : half * 4 + 4] = m
            total[n, half * 4 : half * 4 + 4] = jnp.sum(e, axis=1)
            e = e.astype(jnp.bfloat16)
            for g in range(4):
                h = half * 4 + g
                part[n, h * HS : (h + 1) * HS] = dot(values[h * HS : (h + 1) * HS], e[g])

    for j in ORDER:
        attend3(0, j)

        @pl.loop(1, 8)
        def _(row):
            send(row, j).wait_recv()
            attend3(row, j)

    def spread(i, half):
        group = (y + i) % RING
        return pltpu.make_async_remote_copy(
            src_ref=hid.at[pl.ds(half * 4, 4), pl.ds(group * 64, 64)],
            dst_ref=arr.at[pl.ds(y * 8 + half * 4, 4)],
            send_sem=snap_send.at[half, i],
            recv_sem=snap_recv.at[half, i],
            device_id=(group, lax.axis_index("vert")),
            device_id_type=MESH,
        )

    for half in range(2):

        @pl.loop(half * 4, half * 4 + 4)
        def _(s):
            for u in range(2):
                b = s * 2 + u
                slots, live, tops = [], [], []
                for k in range(KT):
                    slot = table[b, k]
                    alive = slot >= 0
                    slot = jnp.where(alive, slot, 0)
                    slots.append(slot)
                    live.append(jnp.where(alive, jnp.float32(0), jnp.float32(-jnp.inf)))
                    tops.append(top[slot] + live[k])
                m = functools.reduce(jnp.maximum, tops)
                weights = [jnp.exp2(t - m) for t in tops]
                denominator = sum(weights[k] * total[slots[k]] for k in range(KT))
                weights = [w / denominator for w in weights]
                parts = []
                for h in range(HEADS):
                    parts.append(
                        sum(
                            weights[k][h : h + 1] * part[slots[k], h * HS : (h + 1) * HS]
                            for k in range(KT)
                        )
                    )
                attended = jnp.concatenate(parts, axis=0).T.astype(jnp.bfloat16)
                update = dot(attended, wso[...])
                hid[s, u * TILE : (u + 1) * TILE] = (feat[b].astype(jnp.float32) + update).astype(
                    jnp.bfloat16
                )

        for i in (2, 1, 3):
            spread(i, half).start()

    own = pltpu.make_async_copy(hid.at[:, pl.ds(y * 64, 64)], arr.at[pl.ds(y * 8, 8)], own_sem)
    own.start()
    own.wait()
    for half in range(2):
        for i in range(1, RING):
            spread(i, half).wait()
    for j in ORDER:
        if j:
            share(j).wait_send()

        @pl.loop(1, 8)
        def _(row):
            send(row, j).wait_send()


def time_kernel(births, arr, pos, wqkv, wo, out, wt):
    y = lax.axis_index("snap")
    step = pl.program_id(0)

    @pl.when(step == 0)
    def _():
        wt[0] = wqkv[:, :D].astype(jnp.float32).T.astype(jnp.bfloat16)
        wt[1] = wqkv[:, 2 * D :].astype(jnp.float32).T.astype(jnp.bfloat16)

    snaps = pos.shape[0]
    n = snaps * 8
    hidden = arr[...].astype(jnp.float32)
    positions = pos[...].astype(jnp.float32)[:, None, :]
    lane_head = lax.broadcasted_iota(jnp.int32, (1, TILE), 1) // HS
    vertex = lax.broadcasted_iota(jnp.int32, (1, 8, 1), 1)
    lane = lax.broadcasted_iota(jnp.int32, (1, 1, n), 2)
    key_snap = lax.broadcasted_iota(jnp.int32, (snaps, 1, 1), 0)
    for g in range(2):
        base = y * 64 + step * 16 + g * 8
        birth = jnp.zeros((1, 8, 1), jnp.int32)
        for v in range(8):
            birth = jnp.where(vertex == v, births[base + v], birth)
        query_snap = lane // 8
        allowed = (lane % 8 == vertex) & (
            (query_snap == key_snap) | ((query_snap >= key_snap) & (key_snap >= birth))
        )
        bias = jnp.where(allowed, jnp.float32(0), jnp.float32(-jnp.inf)).reshape(n, n)
        mine = hidden[:, g * 8 : (g + 1) * 8]
        rows = (mine + positions).reshape(n, D).astype(jnp.bfloat16)
        q = (dot(wt[0], rows, NT) * SCALE).astype(jnp.bfloat16)
        keys = dot(rows, wqkv[:, D : 2 * D]).astype(jnp.bfloat16)
        values = dot(wt[1], rows, NT).astype(jnp.bfloat16)
        mixed = []
        for h in range(HEADS):
            half = (h // 4) * TILE
            mask = (lane_head == h % 4).astype(jnp.float32).astype(jnp.bfloat16)
            s = dot(keys[:, half : half + TILE] * mask, q[half : half + TILE]) + bias
            m = jnp.max(s, axis=0, keepdims=True)
            e = jnp.exp2(s - m)
            t = jnp.sum(e, axis=0, keepdims=True)
            o = dot(values[h * HS : (h + 1) * HS], e.astype(jnp.bfloat16))
            mixed.append(o / t)
        mixed = jnp.concatenate(mixed, axis=0).T.astype(jnp.bfloat16)
        out[:, g * 8 : (g + 1) * 8] = mine + dot(mixed, wo[...]).reshape(snaps, 8, D)


def local(features, tile_cols, counts, births, wq, wkv, wso, pos, wqkv, wo):
    snaps, rows, width = features.shape
    smem = pl.BlockSpec(memory_space=pltpu.SMEM)
    vmem = pl.BlockSpec(memory_space=pltpu.VMEM)
    hbm = pl.BlockSpec(memory_space=pl.ANY)
    dma = pltpu.SemaphoreType.DMA
    req, blk, table = pl.pallas_call(
        prep_kernel,
        out_shape=(
            jax.ShapeDtypeStruct((8, 128), jnp.int32),
            jax.ShapeDtypeStruct((SLOTS,), jnp.int32),
            jax.ShapeDtypeStruct((BLOCKS, KT), jnp.int32),
        ),
        in_specs=[smem] * 2,
        out_specs=(smem,) * 3,
        scratch_shapes=[pltpu.SMEM((8, RING), jnp.int32)],
        name="rank_entries",
    )(tile_cols.reshape(BLOCKS, KT), counts.reshape(BLOCKS))
    half = jnp.bfloat16
    arrived = pl.pallas_call(
        fetch_kernel,
        out_shape=jax.ShapeDtypeStruct((RING * snaps, rows // RING, width), half),
        in_specs=[smem] * 3 + [vmem] * 5,
        out_specs=hbm,
        scratch_shapes=[
            pltpu.VMEM((8, 1, 128), jnp.int32),
            pltpu.SMEM((8, 1, 128), jnp.int32),
            pltpu.VMEM((BLOCKS, TILE, width), half),
            pltpu.VMEM((BLOCKS, TILE, width), half),
            pltpu.VMEM((BLOCKS, TILE, width), half),
            pltpu.VMEM((8, RING, RANKS, TILE, width), half),
            pltpu.VMEM((8, RING, RANKS, TILE, width), half),
            pltpu.VMEM((BLOCKS, 2, TILE, TILE), half),
            pltpu.VMEM((2, width, width), half),
            pltpu.VMEM((SLOTS, width, TILE), jnp.float32),
            pltpu.VMEM((SLOTS, HEADS, TILE), jnp.float32),
            pltpu.VMEM((SLOTS, HEADS, TILE), jnp.float32),
            pltpu.VMEM((snaps, rows, width), half),
            dma((8,)), dma((8,)), dma, dma((3,)), dma((3,)),
            dma((8, RING)), dma((8, RING)), dma((2, RING)), dma((2, RING)), dma,
        ],
        compiler_params=pltpu.CompilerParams(
            collective_id=0, has_side_effects=True, vmem_limit_bytes=56 * 2**20
        ),
        name="fetch_attend",
    )(req, blk, table, req.reshape(8, 1, 128), features.reshape(BLOCKS, TILE, width), wq, wkv, wso)
    count = rows // RING
    result = pl.pallas_call(
        time_kernel,
        out_shape=jax.ShapeDtypeStruct((RING * snaps, count, width), jnp.float32),
        grid=(count // 16,),
        in_specs=[
            smem,
            pl.BlockSpec((RING * snaps, 16, width), lambda i: (0, i, 0)),
            pl.BlockSpec(pos.shape, lambda i: (0, 0)),
            pl.BlockSpec(wqkv.shape, lambda i: (0, 0)),
            pl.BlockSpec(wo.shape, lambda i: (0, 0)),
        ],
        out_specs=pl.BlockSpec((RING * snaps, 16, width), lambda i: (0, i, 0)),
        scratch_shapes=[pltpu.VMEM((2, width, width), half)],
        compiler_params=pltpu.CompilerParams(vmem_limit_bytes=48 * 2**20),
        name="attend_time",
    )(births, arrived, pos, wqkv, wo)
    return result[:, None, None]


def solution(mesh):
    placed = (
        P("snap", "vert", None), P("snap", "vert", None), P("snap", "vert"), P("vert"),
        P(), P(), P(), P(), P(), P(),
    )
    return jax.shard_map(
        local,
        mesh=mesh,
        in_specs=placed,
        out_specs=P(None, "vert", "snap", None, None),
        check_vma=False,
    )
```

```python
import functools

import jax
import jax.numpy as jnp
from jax import lax
from jax.experimental import pallas as pl
from jax.experimental.pallas import tpu as pltpu
from jax.sharding import PartitionSpec as P

HEADS = 8
TILE = 128
D = 256
HS = D // HEADS
KT = 4
BLOCKS = 16
RING = 4
RANKS = 3
SLOTS = 2 * RING * RING * RANKS
SCALE = 1.4426950408889634 * HS**-0.5
MESH = pl.DeviceIdType.MESH
NT = (((1,), (1,)), ((), ()))
TN = (((0,), (0,)), ((), ()))
NN = (((1,), (0,)), ((), ()))


def dot(a, b, dims=NN):
    return lax.dot_general(a, b, dims, preferred_element_type=jnp.float32)


def vert_id(z, x, core):
    return (z * RING + x) * 2 + core


def position():
    v = lax.axis_index("vert")
    return v // (2 * RING), (v // 2) % RING, v % 2


def make_plan(cols, counts, z, x, core, plan_v):
    shape = (TILE, TILE)
    lane = lax.broadcasted_iota(jnp.int32, (1, TILE), 1)
    col = jnp.full((1, TILE), -1, jnp.int32)
    for n in range(BLOCKS * KT):
        s, u, k = n // 8, (n // 4) % 2, n % 4
        col = jnp.where(lane == n, jnp.where(k < counts[s, u], cols[s, u, k], -1), col)
    owner = jnp.maximum(col, 0) >> 1
    oz, ox, oc = owner >> 3, (owner >> 1) & 3, owner & 1
    i = jnp.where(oc == 0, x - ox, z - oz) & 3
    j = jnp.where(oc == 0, oz - z, ox - x) & 3
    base = (jnp.where(oc == core, 0, RING) + i) * RING + j
    base = jnp.where(col >= 0, base, -1)
    base_down = jnp.broadcast_to(base, shape).T
    n_down = lax.broadcasted_iota(jnp.int32, shape, 0)
    n_across = lax.broadcasted_iota(jnp.int32, shape, 1)
    before = (base_down == base) & (n_down < n_across)
    rank = jnp.sum(jnp.where(before, 1, 0), axis=0, keepdims=True)
    place = jnp.where(base >= 0, base * RANKS + rank, -1)
    place_down = jnp.broadcast_to(place, shape).T
    code = ((lane >> 3) << 1) + (jnp.maximum(col, 0) & 1)
    code_down = jnp.broadcast_to(code, shape).T
    plan_v[16] = place
    per = RING * RANKS
    for row in range(8):
        hit = (place_down == n_across + row * per) & (n_across < per)
        plan_v[row] = jnp.sum(jnp.where(hit, code_down, 0), axis=0, keepdims=True)
        plan_v[8 + row] = jnp.sum(jnp.where(hit, n_down >> 2, 0), axis=0, keepdims=True)


def graph_kernel(
    cols, counts, births, feat, wq_in, wkv_in, wso, pos, wqkv, wo, out,
    plan_v, plan, codes_v, codes, ag1, ag2, ag3, stage, recv, wq, wt, turn_s, part, top, total, hid, arr, held,
    req_send, req_recv, loc_sem, ag_send, ag_recv, tile_send, tile_recv, snap_send, snap_recv, own_sem, out_sem,
):
    z, x, core = position()
    y = lax.axis_index("snap")
    flat = core == 0

    def gather_peer(j):
        return vert_id(
            jnp.where(flat, (z + j) % RING, z), jnp.where(flat, x, (x + j) % RING), core
        )

    def dest(row):
        i = row % RING
        other = row // RING
        return vert_id(
            jnp.where(flat, z, (z + i) % RING),
            jnp.where(flat, (x + i) % RING, x),
            (core + other) % 2,
        )

    def relay(row):
        i = row % RING
        c = (core + row // RING) % 2
        return vert_id(
            jnp.where(c == 0, z, (z + RING - i) % RING),
            jnp.where(c == 0, (x + RING - i) % RING, x),
            c,
        )

    barrier = pltpu.get_barrier_semaphore()
    greet = [gather_peer(1), gather_peer(2), gather_peer(3)]
    greet += [dest(r) for r in range(1, 8)]
    greet += [relay(r) for r in range(5, 8)]
    for v in greet:
        pl.semaphore_signal(barrier, inc=1, device_id=(y, v), device_id_type=MESH)
    for i in range(1, RING):
        pl.semaphore_signal(
            barrier, inc=1, device_id=((y + i) % RING, lax.axis_index("vert")), device_id_type=MESH
        )
    pl.semaphore_wait(barrier, len(greet) + RING - 1)

    gathered = {1: ag1, 2: ag2, 3: ag3}
    lower, upper = pl.ds(0, 8), pl.ds(8, 8)

    def share(j, half):
        rows = upper if half else lower
        source = (ag3 if half else ag1) if j == 2 else feat
        there = gather_peer((1 if half else 3) if j == 2 else RING - j)
        return pltpu.make_async_remote_copy(
            src_ref=source.at[rows],
            dst_ref=gathered[j].at[rows],
            send_sem=ag_send.at[j - 1, half],
            recv_sem=ag_recv.at[j - 1, half],
            device_id=(y, there),
            device_id_type=MESH,
        )

    share(1, 0).start()
    share(3, 1).start()
    share(1, 1).start()
    share(3, 0).start()

    make_plan(cols, counts, z, x, core, plan_v)

    def ask(row):
        return pltpu.make_async_remote_copy(
            src_ref=plan_v.at[row],
            dst_ref=codes_v.at[row],
            send_sem=req_send.at[row],
            recv_sem=req_recv.at[row],
            device_id=(y, relay(row)),
            device_id_type=MESH,
        )

    for row in range(1, 8):
        ask(row).start()
    mine_down = pltpu.make_async_copy(plan_v, plan, own_sem)
    mine_down.start()

    wt[0] = wq_in[...].astype(jnp.float32).T.astype(jnp.bfloat16)
    wt[1] = wkv_in[:, D:].astype(jnp.float32).T.astype(jnp.bfloat16)

    @pl.loop(0, BLOCKS)
    def _(b):
        q = (dot(wt[0], feat[b], NT) * SCALE).astype(jnp.bfloat16)
        wq[b, 0] = q[:TILE]
        wq[b, 1] = q[TILE:]

    mine_down.wait()
    for row in range(1, 8):
        ask(row).wait()
    down = pltpu.make_async_copy(codes_v.at[pl.ds(1, 7)], codes.at[pl.ds(1, 7)], loc_sem)
    down.start()
    down.wait()

    def send(row, j):
        return pltpu.make_async_remote_copy(
            src_ref=stage.at[row, j],
            dst_ref=recv.at[row, j],
            send_sem=tile_send.at[row, j],
            recv_sem=tile_recv.at[row, j],
            device_id=(y, dest(row)),
            device_id_type=MESH,
        )

    def pass_on(j):
        source = gathered[j] if j else feat

        @pl.loop(1, 8)
        def _(row):
            for r in range(RANKS):
                stage[row, j, r] = source[codes[row, 0, j * RANKS + r]]
            send(row, j).start()

        for r in range(RANKS):
            recv[0, j, r] = source[plan[0, 0, j * RANKS + r]]

    lane_head = lax.broadcasted_iota(jnp.int32, (1, TILE), 1) // HS
    masks = [(lane_head == g).astype(jnp.float32).astype(jnp.bfloat16) for g in range(4)]

    def attend3(row, j):
        rows3 = recv[row, j].reshape(RANKS * TILE, D)
        keys3 = dot(rows3, wkv_in[:, :D]).astype(jnp.bfloat16)
        values3 = dot(wt[1], rows3, NT).astype(jnp.bfloat16)
        for r in range(RANKS):
            attend(row, j, r, keys3[r * TILE : (r + 1) * TILE], values3[:, r * TILE : (r + 1) * TILE])

    def attend(row, j, r, keys, values):
        n = (row * RING + j) * RANKS + r
        b = plan[8 + row, 0, j * RANKS + r]

        for half in range(2):
            kh = keys[:, half * TILE : (half + 1) * TILE]
            s = dot(jnp.concatenate([kh * w for w in masks], axis=0), wq[b, half])
            s = s.reshape(4, TILE, TILE)
            m = jnp.max(s, axis=1)
            e = jnp.exp2(s - m[:, None])
            top[n, half * 4 : half * 4 + 4] = m
            total[n, half * 4 : half * 4 + 4] = jnp.sum(e, axis=1)
            e = e.astype(jnp.bfloat16)
            for g in range(4):
                h = half * 4 + g
                part[n, h * HS : (h + 1) * HS] = dot(values[h * HS : (h + 1) * HS], e[g])

    def attend_rows(j, first, last):
        @pl.loop(first, last)
        def _(row):
            send(row, j).wait_recv()
            attend3(row, j)

    def attend_own(j):
        @pl.loop(0, 1)
        def _(row):
            attend3(row, j)

    pass_on(0)
    share(1, 0).wait_recv()
    share(2, 0).start()
    share(3, 1).wait_recv()
    share(2, 1).start()
    attend_own(0)
    share(1, 1).wait_recv()
    pass_on(1)
    share(3, 0).wait_recv()
    pass_on(3)
    attend_own(1)
    attend_own(3)
    attend_rows(0, 1, 4)
    share(2, 0).wait_recv()
    share(2, 1).wait_recv()
    pass_on(2)

    wt[2] = wqkv[:, :D].astype(jnp.float32).T.astype(jnp.bfloat16)
    wt[3] = wqkv[:, 2 * D :].astype(jnp.float32).T.astype(jnp.bfloat16)
    snaps = pos.shape[0]
    n = snaps * 8
    to = lax.broadcasted_iota(jnp.int32, (n, n), 0)
    source = lax.broadcasted_iota(jnp.int32, (n, n), 1)
    turn_s[0] = ((to % snaps) * 8 + to // snaps == source).astype(jnp.float32).astype(jnp.bfloat16)
    turn_s[1] = ((source % snaps) * 8 + source // snaps == to).astype(jnp.float32).astype(jnp.bfloat16)

    attend_rows(0, 4, 8)
    attend_own(2)
    attend_rows(1, 1, 8)
    attend_rows(3, 1, 8)
    attend_rows(2, 1, 8)

    @pl.loop(0, 8)
    def _(s):
        for u in range(2):
            b = s * 2 + u
            slots, live, tops = [], [], []
            for k in range(KT):
                slot = plan[16, 0, b * KT + k]
                alive = slot >= 0
                slot = jnp.where(alive, slot, 0)
                slots.append(slot)
                live.append(jnp.where(alive, jnp.float32(0), jnp.float32(-jnp.inf)))
                tops.append(top[slot] + live[k])
            m = functools.reduce(jnp.maximum, tops)
            weights = [jnp.exp2(t - m) for t in tops]
            denominator = sum(weights[k] * total[slots[k]] for k in range(KT))
            weights = [w / denominator for w in weights]
            parts = []
            for h in range(HEADS):
                parts.append(
                    sum(
                        weights[k][h : h + 1] * part[slots[k], h * HS : (h + 1) * HS]
                        for k in range(KT)
                    )
                )
            attended = jnp.concatenate(parts, axis=0).T.astype(jnp.bfloat16)
            update = dot(attended, wso[...])
            hid[s, u * TILE : (u + 1) * TILE] = (feat[b].astype(jnp.float32) + update).astype(
                jnp.bfloat16
            )


    def spread(i, chunk):
        group = (y + i) % RING
        return pltpu.make_async_remote_copy(
            src_ref=hid.at[:, pl.ds(group * 64 + chunk * 16, 16)],
            dst_ref=arr.at[pl.ds(y * 8, 8), pl.ds(chunk * 16, 16)],
            send_sem=snap_send.at[chunk, i],
            recv_sem=snap_recv.at[chunk, i],
            device_id=(group, lax.axis_index("vert")),
            device_id_type=MESH,
        )

    for chunk in range(4):
        for i in (2, 1, 3):
            spread(i, chunk).start()
    arr[pl.ds(y * 8, 8)] = hid[:, pl.ds(y * 64, 64)]

    lane = lax.broadcasted_iota(jnp.int32, (1, 1, TILE), 2)
    key_snap = lax.broadcasted_iota(jnp.int32, (1, snaps, 1), 1)
    query_snap = lane % snaps
    own_lane = [lane // snaps == v for v in range(4)]
    positions = pos[...].astype(jnp.float32)[:, None, :]

    def write(step):
        return pltpu.make_async_copy(held.at[step], out.at[:, pl.ds(step * 16, 16)], out_sem.at[step])

    @pl.loop(0, 4)
    def _(step):
        for i in range(1, RING):
            spread(i, step).wait_recv()
        hidden = arr[:, pl.ds(step * 16, 16)].astype(jnp.float32)
        for g in range(2):
            base = y * 64 + step * 16 + g * 8
            mine = hidden[:, g * 8 : (g + 1) * 8]
            rows = (mine + positions).reshape(n, D).astype(jnp.bfloat16)
            rows = dot(turn_s[0], rows).astype(jnp.bfloat16)
            q = (dot(wt[2], rows, NT) * SCALE).astype(jnp.bfloat16)
            keys = dot(rows, wqkv[:, D : 2 * D]).astype(jnp.bfloat16)
            values = dot(wt[3], rows, NT).astype(jnp.bfloat16)
            sides = []
            for u in range(2):
                birth = jnp.zeros((1, 1, TILE), jnp.int32)
                for v in range(4):
                    birth = jnp.where(own_lane[v], births[base + u * 4 + v], birth)
                allowed = (query_snap == key_snap) | ((query_snap >= key_snap) & (key_snap >= birth))
                bias = jnp.where(allowed, jnp.float32(0), jnp.float32(-jnp.inf))
                mixed = []
                for half in range(2):
                    kh = keys[u * TILE : (u + 1) * TILE, half * TILE : (half + 1) * TILE]
                    qh = q[half * TILE : (half + 1) * TILE, u * TILE : (u + 1) * TILE]
                    s = dot(jnp.concatenate([kh * w for w in masks], axis=0), qh)
                    s = s.reshape(4, 4, snaps, TILE)
                    near = s[:, 0]
                    for v in range(1, 4):
                        near = jnp.where(own_lane[v], s[:, v], near)
                    near = near + bias
                    m = jnp.max(near, axis=1, keepdims=True)
                    e = jnp.exp2(near - m)
                    t = jnp.sum(e, axis=1, keepdims=True)
                    for h in range(4):
                        wide = jnp.concatenate(
                            [jnp.where(own_lane[v][0], e[h], 0.0) for v in range(4)], axis=0
                        ).astype(jnp.bfloat16)
                        top = (half * 4 + h) * HS
                        o = dot(values[top : top + HS, u * TILE : (u + 1) * TILE], wide)
                        mixed.append((o / t[h]).astype(jnp.bfloat16))
                sides.append(jnp.concatenate(mixed, axis=0))
            mixed = dot(turn_s[1], jnp.concatenate(sides, axis=1), NT).astype(jnp.bfloat16)
            held[step, :, g * 8 : (g + 1) * 8] = mine + dot(mixed, wo[...]).reshape(snaps, 8, D)
        write(step).start()

    for chunk in range(4):
        write(chunk).wait()
        for i in range(1, RING):
            spread(i, chunk).wait_send()
    for j, half in ((1, 0), (1, 1), (2, 0), (2, 1), (3, 0), (3, 1)):
        share(j, half).wait_send()
    for j in range(RING):

        @pl.loop(1, 8)
        def _(row):
            send(row, j).wait_send()


def local(features, tile_cols, counts, births, wq, wkv, wso, pos, wqkv, wo):
    snaps, rows, width = features.shape
    smem = pl.BlockSpec(memory_space=pltpu.SMEM)
    vmem = pl.BlockSpec(memory_space=pltpu.VMEM)
    dma = pltpu.SemaphoreType.DMA
    half = jnp.bfloat16
    count = rows // RING
    result = pl.pallas_call(
        graph_kernel,
        out_shape=jax.ShapeDtypeStruct((RING * snaps, count, width), jnp.float32),
        in_specs=[smem] * 3 + [vmem] * 7,
        out_specs=pl.BlockSpec(memory_space=pl.ANY),
        scratch_shapes=[
            pltpu.VMEM((17, 1, TILE), jnp.int32),
            pltpu.SMEM((17, 1, TILE), jnp.int32),
            pltpu.VMEM((8, 1, TILE), jnp.int32),
            pltpu.SMEM((8, 1, TILE), jnp.int32),
            pltpu.VMEM((BLOCKS, TILE, width), half),
            pltpu.VMEM((BLOCKS, TILE, width), half),
            pltpu.VMEM((BLOCKS, TILE, width), half),
            pltpu.VMEM((8, RING, RANKS, TILE, width), half),
            pltpu.VMEM((8, RING, RANKS, TILE, width), half),
            pltpu.VMEM((BLOCKS, 2, TILE, TILE), half),
            pltpu.VMEM((4, width, width), half),
            pltpu.VMEM((2, RING * snaps * 8, RING * snaps * 8), half),
            pltpu.VMEM((SLOTS, width, TILE), jnp.float32),
            pltpu.VMEM((SLOTS, HEADS, TILE), jnp.float32),
            pltpu.VMEM((SLOTS, HEADS, TILE), jnp.float32),
            pltpu.VMEM((snaps, rows, width), half),
            pltpu.VMEM((RING * snaps, count, width), half),
            pltpu.VMEM((RING, RING * snaps, 16, width), jnp.float32),
            dma((8,)), dma((8,)), dma, dma((3, 2)), dma((3, 2)),
            dma((8, RING)), dma((8, RING)), dma((4, RING)), dma((4, RING)), dma, dma((4,)),
        ],
        compiler_params=pltpu.CompilerParams(
            collective_id=0, has_side_effects=True, vmem_limit_bytes=56 * 2**20
        ),
        name="graph",
    )(tile_cols, counts, births, features.reshape(BLOCKS, TILE, width), wq, wkv, wso, pos, wqkv, wo)
    return result[:, None, None]


def solution(mesh):
    placed = (
        P("snap", "vert", None), P("snap", "vert", None), P("snap", "vert"), P("vert"),
        P(), P(), P(), P(), P(), P(),
    )
    return jax.shard_map(
        local,
        mesh=mesh,
        in_specs=placed,
        out_specs=P(None, "vert", "snap", None, None),
        check_vma=False,
    )
```

```python
import functools

import jax
import jax.numpy as jnp
from jax import lax
from jax.experimental import pallas as pl
from jax.experimental.pallas import tpu as pltpu
from jax.sharding import PartitionSpec as P

HEADS = 8
TILE = 128
D = 256
HS = D // HEADS
KT = 4
BLOCKS = 16
RING = 4
RANKS = 3
SLOTS = 2 * RING * RING * RANKS
SCALE = 1.4426950408889634 * HS**-0.5
MESH = pl.DeviceIdType.MESH
NT = (((1,), (1,)), ((), ()))
TN = (((0,), (0,)), ((), ()))
NN = (((1,), (0,)), ((), ()))


def dot(a, b, dims=NN):
    return lax.dot_general(a, b, dims, preferred_element_type=jnp.float32)


def vert_id(z, x, core):
    return (z * RING + x) * 2 + core


def position():
    v = lax.axis_index("vert")
    return v // (2 * RING), (v // 2) % RING, v % 2


def make_plan(cols, counts, z, x, core, plan_v):
    shape = (TILE, TILE)
    lane = lax.broadcasted_iota(jnp.int32, (1, TILE), 1)
    col = jnp.full((1, TILE), -1, jnp.int32)
    for n in range(BLOCKS * KT):
        s, u, k = n // 8, (n // 4) % 2, n % 4
        col = jnp.where(lane == n, jnp.where(k < counts[u, s], cols[u, k, s], -1), col)
    owner = jnp.maximum(col, 0) >> 1
    oz, ox, oc = owner >> 3, (owner >> 1) & 3, owner & 1
    i = jnp.where(oc == 0, x - ox, z - oz) & 3
    j = jnp.where(oc == 0, oz - z, ox - x) & 3
    base = (jnp.where(oc == core, 0, RING) + i) * RING + j
    base = jnp.where(col >= 0, base, -1)
    base_down = jnp.broadcast_to(base, shape).T
    n_down = lax.broadcasted_iota(jnp.int32, shape, 0)
    n_across = lax.broadcasted_iota(jnp.int32, shape, 1)
    before = (base_down == base) & (n_down < n_across)
    rank = jnp.sum(jnp.where(before, 1, 0), axis=0, keepdims=True)
    place = jnp.where(base >= 0, base * RANKS + rank, -1)
    place_down = jnp.broadcast_to(place, shape).T
    code = ((lane >> 3) << 1) + (jnp.maximum(col, 0) & 1)
    code_down = jnp.broadcast_to(code, shape).T
    plan_v[16] = place
    per = RING * RANKS
    for row in range(8):
        hit = (place_down == n_across + row * per) & (n_across < per)
        plan_v[row] = jnp.sum(jnp.where(hit, code_down, 0), axis=0, keepdims=True)
        plan_v[8 + row] = jnp.sum(jnp.where(hit, n_down >> 2, 0), axis=0, keepdims=True)


def graph_kernel(
    cols_in, counts_in, births_in, feat_in, wq_hbm, wkv_hbm, wso_hbm, pos_hbm, wqkv_hbm, wo_hbm, out,
    cols, counts, births, feat, wq_in, wkv_in, wso, pos, wqkv, wo,
    plan_v, plan, codes_v, codes, ag1, ag2, ag3, stage, recv, wq, wt, turn_s, part, top, total, hid, arr, held,
    req_send, req_recv, loc_sem, ag_send, ag_recv, tile_send, tile_recv, snap_send, snap_recv, own_sem, out_sem, in_sem,
):
    z, x, core = position()
    y = lax.axis_index("snap")
    flat = core == 0

    def gather_peer(j):
        return vert_id(
            jnp.where(flat, (z + j) % RING, z), jnp.where(flat, x, (x + j) % RING), core
        )

    def dest(row):
        i = row % RING
        other = row // RING
        return vert_id(
            jnp.where(flat, z, (z + i) % RING),
            jnp.where(flat, (x + i) % RING, x),
            (core + other) % 2,
        )

    def relay(row):
        i = row % RING
        c = (core + row // RING) % 2
        return vert_id(
            jnp.where(c == 0, z, (z + RING - i) % RING),
            jnp.where(c == 0, (x + RING - i) % RING, x),
            c,
        )

    held_here = [
        pltpu.make_async_copy(there, here, in_sem.at[at])
        for at, (there, here) in enumerate(
            (
                (cols_in, cols), (counts_in, counts), (births_in, births), (wq_hbm, wq_in), (feat_in, feat),
                (wkv_hbm, wkv_in), (wso_hbm, wso), (pos_hbm, pos), (wqkv_hbm, wqkv), (wo_hbm, wo),
            )
        )
    ]
    for copy in held_here:
        copy.start()
    barrier = pltpu.get_barrier_semaphore()
    greet = [gather_peer(1), gather_peer(2), gather_peer(3)]
    greet += [dest(r) for r in range(1, 8)]
    greet += [relay(r) for r in range(5, 8)]
    for v in greet:
        pl.semaphore_signal(barrier, inc=1, device_id=(y, v), device_id_type=MESH)
    for i in range(1, RING):
        pl.semaphore_signal(
            barrier, inc=1, device_id=((y + i) % RING, lax.axis_index("vert")), device_id_type=MESH
        )
    held_here[0].wait()
    held_here[1].wait()
    make_plan(cols, counts, z, x, core, plan_v)
    pl.semaphore_wait(barrier, len(greet) + RING - 1)

    def ask(row):
        return pltpu.make_async_remote_copy(
            src_ref=plan_v.at[row],
            dst_ref=codes_v.at[row],
            send_sem=req_send.at[row],
            recv_sem=req_recv.at[row],
            device_id=(y, relay(row)),
            device_id_type=MESH,
        )

    for row in range(1, 8):
        ask(row).start()

    gathered = {1: ag1, 2: ag2, 3: ag3}
    lower, upper = pl.ds(0, 8), pl.ds(8, 8)

    def share(j, half):
        rows = upper if half else lower
        source = (ag3 if half else ag1) if j == 2 else feat_in
        there = gather_peer((1 if half else 3) if j == 2 else RING - j)
        return pltpu.make_async_remote_copy(
            src_ref=source.at[rows],
            dst_ref=gathered[j].at[rows],
            send_sem=ag_send.at[j - 1, half],
            recv_sem=ag_recv.at[j - 1, half],
            device_id=(y, there),
            device_id_type=MESH,
        )

    share(1, 0).start()
    share(3, 1).start()
    share(1, 1).start()
    share(3, 0).start()

    mine_down = pltpu.make_async_copy(plan_v, plan, own_sem)
    mine_down.start()

    mine_down.wait()
    for row in range(1, 8):
        ask(row).wait()
    down = pltpu.make_async_copy(codes_v.at[pl.ds(1, 7)], codes.at[pl.ds(1, 7)], loc_sem)
    down.start()
    down.wait()

    def send(row, j):
        return pltpu.make_async_remote_copy(
            src_ref=stage.at[row, j],
            dst_ref=recv.at[row, j],
            send_sem=tile_send.at[row, j],
            recv_sem=tile_recv.at[row, j],
            device_id=(y, dest(row)),
            device_id_type=MESH,
        )

    def pass_on(j):
        source = gathered[j] if j else feat

        @pl.loop(1, 8)
        def _(row):
            for r in range(RANKS):
                stage[row, j, r] = source[codes[row, 0, j * RANKS + r]]
            send(row, j).start()

        for r in range(RANKS):
            recv[0, j, r] = source[plan[0, 0, j * RANKS + r]]

    lane_head = lax.broadcasted_iota(jnp.int32, (1, TILE), 1) // HS
    masks = [(lane_head == g).astype(jnp.float32).astype(jnp.bfloat16) for g in range(4)]

    def attend3(row, j):
        rows3 = recv[row, j].reshape(RANKS * TILE, D)
        keys3 = dot(rows3, wkv_in[:, :D]).astype(jnp.bfloat16)
        values3 = dot(wt[1], rows3, NT).astype(jnp.bfloat16)
        for r in range(RANKS):
            attend(row, j, r, keys3[r * TILE : (r + 1) * TILE], values3[:, r * TILE : (r + 1) * TILE])

    def attend(row, j, r, keys, values):
        n = (row * RING + j) * RANKS + r
        b = plan[8 + row, 0, j * RANKS + r]

        for g in range(4):
            s = dot(keys * jnp.concatenate([masks[g], masks[g]], axis=1), wq[b])
            m = jnp.max(s, axis=0, keepdims=True)
            e = jnp.exp2(s - m)
            t = jnp.sum(e, axis=0, keepdims=True)
            e = e.astype(jnp.bfloat16)
            for half in range(2):
                lanes = slice(half * TILE, (half + 1) * TILE)
                h = half * 4 + g
                top[n, h : h + 1] = m[:, lanes]
                total[n, h : h + 1] = t[:, lanes]
                part[n, h * HS : (h + 1) * HS] = dot(values[h * HS : (h + 1) * HS], e[:, lanes])

    def turn_of(t):
        k = jnp.maximum(t - 8, 0)
        pair = (k % 6) // 2
        far = jnp.where(pair == 0, 1, jnp.where(pair == 1, 3, 2)) + RING * (k % 2)
        near = jnp.where((t < 3) | (t == 6), 0, RING)
        row = jnp.where(t < 8, near, far)
        order = jnp.where(t < 3, t, jnp.where(t < 6, t - 3, jnp.where(t < 8, 3, k // 6)))
        return row, jnp.where(order == 2, 3, jnp.where(order == 3, 2, order))

    def attend_span(first, last):
        @pl.loop(first, last)
        def _(t):
            row, j = turn_of(t)

            @pl.when(row != 0)
            def _():
                send(row, j).wait_recv()

            attend3(row, j)

    for copy in held_here[2:]:
        copy.wait()

    wt[0] = wq_in[...].astype(jnp.float32).T.astype(jnp.bfloat16)
    wt[1] = wkv_in[:, D:].astype(jnp.float32).T.astype(jnp.bfloat16)

    @pl.loop(0, BLOCKS)
    def _(b):
        q = (dot(wt[0], feat[b], NT) * SCALE).astype(jnp.bfloat16)
        wq[b, :TILE, :TILE] = q[:TILE]
        wq[b, :TILE, TILE:] = jnp.zeros((TILE, TILE), jnp.bfloat16)
        wq[b, TILE:, :TILE] = jnp.zeros((TILE, TILE), jnp.bfloat16)
        wq[b, TILE:, TILE:] = q[TILE:]

    share(1, 0).wait_recv()
    share(2, 0).start()
    share(3, 1).wait_recv()
    share(2, 1).start()
    share(1, 1).wait_recv()
    share(3, 0).wait_recv()
    pass_on(0)
    pass_on(1)
    pass_on(3)
    attend_span(0, 3)
    share(2, 0).wait_recv()
    share(2, 1).wait_recv()
    pass_on(2)

    wt[2] = wqkv[:, :D].astype(jnp.float32).T.astype(jnp.bfloat16)
    wt[3] = wqkv[:, 2 * D :].astype(jnp.float32).T.astype(jnp.bfloat16)
    snaps = pos.shape[0]
    n = snaps * 8
    to = lax.broadcasted_iota(jnp.int32, (n, n), 0)
    source = lax.broadcasted_iota(jnp.int32, (n, n), 1)
    turn_s[0] = ((to % snaps) * 8 + to // snaps == source).astype(jnp.float32).astype(jnp.bfloat16)
    turn_s[1] = ((source % snaps) * 8 + source // snaps == to).astype(jnp.float32).astype(jnp.bfloat16)

    attend_span(3, 32)

    @pl.loop(0, 8)
    def _(s):
        for u in range(2):
            b = s * 2 + u
            slots, live, tops = [], [], []
            for k in range(KT):
                slot = plan[16, 0, b * KT + k]
                alive = slot >= 0
                slot = jnp.where(alive, slot, 0)
                slots.append(slot)
                live.append(jnp.where(alive, jnp.float32(0), jnp.float32(-jnp.inf)))
                tops.append(top[slot] + live[k])
            m = functools.reduce(jnp.maximum, tops)
            weights = [jnp.exp2(t - m) for t in tops]
            denominator = sum(weights[k] * total[slots[k]] for k in range(KT))
            weights = [w / denominator for w in weights]
            parts = []
            for h in range(HEADS):
                parts.append(
                    sum(
                        weights[k][h : h + 1] * part[slots[k], h * HS : (h + 1) * HS]
                        for k in range(KT)
                    )
                )
            attended = jnp.concatenate(parts, axis=0).T.astype(jnp.bfloat16)
            update = dot(attended, wso[...])
            hid[s, u * TILE : (u + 1) * TILE] = (feat[b].astype(jnp.float32) + update).astype(
                jnp.bfloat16
            )


    def spread(i, chunk):
        group = (y + i) % RING
        return pltpu.make_async_remote_copy(
            src_ref=hid.at[:, pl.ds(group * 64 + chunk * 16, 16)],
            dst_ref=arr.at[pl.ds(y * 8, 8), pl.ds(chunk * 16, 16)],
            send_sem=snap_send.at[chunk, i],
            recv_sem=snap_recv.at[chunk, i],
            device_id=(group, lax.axis_index("vert")),
            device_id_type=MESH,
        )

    for chunk in range(4):
        for i in (2, 1, 3):
            spread(i, chunk).start()
    arr[pl.ds(y * 8, 8)] = hid[:, pl.ds(y * 64, 64)]

    lane = lax.broadcasted_iota(jnp.int32, (1, 1, TILE), 2)
    key_snap = lax.broadcasted_iota(jnp.int32, (1, snaps, 1), 1)
    query_snap = lane % snaps
    own_lane = [lane // snaps == v for v in range(4)]
    positions = pos[...].astype(jnp.float32)[:, None, :]

    def write(step):
        return pltpu.make_async_copy(held.at[step], out.at[:, pl.ds(step * 16, 16)], out_sem.at[step])

    @pl.loop(0, 4)
    def _(step):
        for i in range(1, RING):
            spread(i, step).wait_recv()
        hidden = arr[:, pl.ds(step * 16, 16)].astype(jnp.float32)
        for g in range(2):
            base = y * 64 + step * 16 + g * 8
            mine = hidden[:, g * 8 : (g + 1) * 8]
            rows = (mine + positions).reshape(n, D).astype(jnp.bfloat16)
            rows = dot(turn_s[0], rows).astype(jnp.bfloat16)
            q = (dot(wt[2], rows, NT) * SCALE).astype(jnp.bfloat16)
            keys = dot(rows, wqkv[:, D : 2 * D]).astype(jnp.bfloat16)
            values = dot(wt[3], rows, NT).astype(jnp.bfloat16)
            sides = []
            for u in range(2):
                birth = jnp.zeros((1, 1, TILE), jnp.int32)
                for v in range(4):
                    birth = jnp.where(own_lane[v], births[base + u * 4 + v], birth)
                allowed = (query_snap == key_snap) | ((query_snap >= key_snap) & (key_snap >= birth))
                bias = jnp.where(allowed, jnp.float32(0), jnp.float32(-jnp.inf))
                mixed = []
                for half in range(2):
                    kh = keys[u * TILE : (u + 1) * TILE, half * TILE : (half + 1) * TILE]
                    qh = q[half * TILE : (half + 1) * TILE, u * TILE : (u + 1) * TILE]
                    s = dot(jnp.concatenate([kh * w for w in masks], axis=0), qh)
                    s = s.reshape(4, 4, snaps, TILE)
                    near = s[:, 0]
                    for v in range(1, 4):
                        near = jnp.where(own_lane[v], s[:, v], near)
                    near = near + bias
                    m = jnp.max(near, axis=1, keepdims=True)
                    e = jnp.exp2(near - m)
                    t = jnp.sum(e, axis=1, keepdims=True)
                    for h in range(4):
                        wide = jnp.concatenate(
                            [jnp.where(own_lane[v][0], e[h], 0.0) for v in range(4)], axis=0
                        ).astype(jnp.bfloat16)
                        top = (half * 4 + h) * HS
                        o = dot(values[top : top + HS, u * TILE : (u + 1) * TILE], wide)
                        mixed.append((o / t[h]).astype(jnp.bfloat16))
                sides.append(jnp.concatenate(mixed, axis=0))
            mixed = dot(turn_s[1], jnp.concatenate(sides, axis=1), NT).astype(jnp.bfloat16)
            held[step, :, g * 8 : (g + 1) * 8] = mine + dot(mixed, wo[...]).reshape(snaps, 8, D)
        write(step).start()

    for chunk in range(4):
        write(chunk).wait()
        for i in range(1, RING):
            spread(i, chunk).wait_send()
    for j, half in ((1, 0), (1, 1), (2, 0), (2, 1), (3, 0), (3, 1)):
        share(j, half).wait_send()
    for j in range(RING):

        @pl.loop(1, 8)
        def _(row):
            send(row, j).wait_send()


def local(features, tile_cols, counts, births, wq, wkv, wso, pos, wqkv, wo):
    snaps, rows, width = features.shape
    hbm = pl.BlockSpec(memory_space=pltpu.HBM)
    dma = pltpu.SemaphoreType.DMA
    half = jnp.bfloat16
    count = rows // RING
    result = pl.pallas_call(
        graph_kernel,
        out_shape=jax.ShapeDtypeStruct((RING * snaps, count, width), jnp.float32),
        in_specs=[hbm] * 10,
        out_specs=pl.BlockSpec(memory_space=pl.ANY),
        scratch_shapes=[
            pltpu.SMEM((rows // TILE, KT, snaps), jnp.int32),
            pltpu.SMEM((rows // TILE, snaps), jnp.int32),
            pltpu.SMEM(births.shape, jnp.int32),
            pltpu.VMEM((BLOCKS, TILE, width), half),
            pltpu.VMEM(wq.shape, half),
            pltpu.VMEM(wkv.shape, half),
            pltpu.VMEM(wso.shape, half),
            pltpu.VMEM(pos.shape, half),
            pltpu.VMEM(wqkv.shape, half),
            pltpu.VMEM(wo.shape, half),
            pltpu.VMEM((17, 1, TILE), jnp.int32),
            pltpu.SMEM((17, 1, TILE), jnp.int32),
            pltpu.VMEM((8, 1, TILE), jnp.int32),
            pltpu.SMEM((8, 1, TILE), jnp.int32),
            pltpu.VMEM((BLOCKS, TILE, width), half),
            pltpu.VMEM((BLOCKS, TILE, width), half),
            pltpu.VMEM((BLOCKS, TILE, width), half),
            pltpu.VMEM((8, RING, RANKS, TILE, width), half),
            pltpu.VMEM((8, RING, RANKS, TILE, width), half),
            pltpu.VMEM((BLOCKS, width, width), half),
            pltpu.VMEM((4, width, width), half),
            pltpu.VMEM((2, RING * snaps * 8, RING * snaps * 8), half),
            pltpu.VMEM((SLOTS, width, TILE), jnp.float32),
            pltpu.VMEM((SLOTS, HEADS, TILE), jnp.float32),
            pltpu.VMEM((SLOTS, HEADS, TILE), jnp.float32),
            pltpu.VMEM((snaps, rows, width), half),
            pltpu.VMEM((RING * snaps, count, width), half),
            pltpu.VMEM((RING, RING * snaps, 16, width), jnp.float32),
            dma((8,)), dma((8,)), dma, dma((3, 2)), dma((3, 2)),
            dma((8, RING)), dma((8, RING)), dma((4, RING)), dma((4, RING)), dma, dma((4,)), dma((10,)),
        ],
        compiler_params=pltpu.CompilerParams(
            collective_id=0, has_side_effects=True, vmem_limit_bytes=58 * 2**20
        ),
        name="graph",
    )(tile_cols.transpose(1, 2, 0), counts.T, births, features.reshape(BLOCKS, TILE, width), wq, wkv, wso, pos, wqkv, wo)
    return result[:, None, None]


def solution(mesh):
    placed = (
        P("snap", "vert", None), P("snap", "vert", None), P("snap", "vert"), P("vert"),
        P(), P(), P(), P(), P(), P(),
    )
    return jax.shard_map(
        local,
        mesh=mesh,
        in_specs=placed,
        out_specs=P(None, "vert", "snap", None, None),
        check_vma=False,
    )
```

```python
import functools

import jax
import jax.numpy as jnp
from jax import lax
from jax.experimental import pallas as pl
from jax.experimental.pallas import tpu as pltpu
from jax.sharding import PartitionSpec as P

HEADS = 8
TILE = 128
D = 256
HS = D // HEADS
KT = 4
BLOCKS = 16
RING = 4
RANKS = 3
SLOTS = 2 * RING * RING * RANKS
SCALE = 1.4426950408889634 * HS**-0.5
MESH = pl.DeviceIdType.MESH
NT = (((1,), (1,)), ((), ()))
TN = (((0,), (0,)), ((), ()))
NN = (((1,), (0,)), ((), ()))


def dot(a, b, dims=NN):
    return lax.dot_general(a, b, dims, preferred_element_type=jnp.float32)


def vert_id(z, x, core):
    return (z * RING + x) * 2 + core


def position():
    v = lax.axis_index("vert")
    return v // (2 * RING), (v // 2) % RING, v % 2


def make_plan(cols, counts, z, x, core, plan_v):
    shape = (TILE, TILE)
    lane = lax.broadcasted_iota(jnp.int32, (1, TILE), 1)
    col = jnp.full((1, TILE), -1, jnp.int32)
    for n in range(BLOCKS * KT):
        s, u, k = n // 8, (n // 4) % 2, n % 4
        col = jnp.where(lane == n, jnp.where(k < counts[u, s], cols[u, k, s], -1), col)
    owner = jnp.maximum(col, 0) >> 1
    oz, ox, oc = owner >> 3, (owner >> 1) & 3, owner & 1
    i = jnp.where(oc == 0, x - ox, z - oz) & 3
    j = jnp.where(oc == 0, oz - z, ox - x) & 3
    base = (jnp.where(oc == core, 0, RING) + i) * RING + j
    base = jnp.where(col >= 0, base, -1)
    base_down = jnp.broadcast_to(base, shape).T
    n_down = lax.broadcasted_iota(jnp.int32, shape, 0)
    n_across = lax.broadcasted_iota(jnp.int32, shape, 1)
    before = (base_down == base) & (n_down < n_across)
    rank = jnp.sum(jnp.where(before, 1, 0), axis=0, keepdims=True)
    place = jnp.where(base >= 0, base * RANKS + rank, -1)
    place_down = jnp.broadcast_to(place, shape).T
    code = ((lane >> 3) << 1) + (jnp.maximum(col, 0) & 1)
    code_down = jnp.broadcast_to(code, shape).T
    plan_v[16] = place
    per = RING * RANKS
    for row in range(8):
        hit = (place_down == n_across + row * per) & (n_across < per)
        plan_v[row] = jnp.sum(jnp.where(hit, code_down, 0), axis=0, keepdims=True)
        plan_v[8 + row] = jnp.sum(jnp.where(hit, n_down >> 2, 0), axis=0, keepdims=True)


def graph_kernel(
    cols_in, counts_in, births_in, feat_in, wq_hbm, wkv_hbm, wso_hbm, pos_hbm, wqkv_hbm, wo_hbm, out,
    cols, counts, births, feat, wq_in, wkv_in, wso, pos, wqkv, wo,
    plan_v, plan, codes_v, codes, ag1, ag2, ag3, stage, recv, wq, wt, turn_s, part, top, total, hid, arr, held,
    req_send, req_recv, loc_sem, ag_send, ag_recv, tile_send, tile_recv, snap_send, snap_recv, own_sem, out_sem, in_sem,
):
    z, x, core = position()
    y = lax.axis_index("snap")
    flat = core == 0

    def gather_peer(j):
        return vert_id(
            jnp.where(flat, (z + j) % RING, z), jnp.where(flat, x, (x + j) % RING), core
        )

    def dest(row):
        i = row % RING
        other = row // RING
        return vert_id(
            jnp.where(flat, z, (z + i) % RING),
            jnp.where(flat, (x + i) % RING, x),
            (core + other) % 2,
        )

    def relay(row):
        i = row % RING
        c = (core + row // RING) % 2
        return vert_id(
            jnp.where(c == 0, z, (z + RING - i) % RING),
            jnp.where(c == 0, (x + RING - i) % RING, x),
            c,
        )

    held_here = [
        pltpu.make_async_copy(there, here, in_sem.at[at])
        for at, (there, here) in enumerate(
            (
                (cols_in, cols), (counts_in, counts), (births_in, births), (wq_hbm, wq_in), (feat_in, feat),
                (wkv_hbm, wkv_in), (wso_hbm, wso), (pos_hbm, pos), (wqkv_hbm, wqkv), (wo_hbm, wo),
            )
        )
    ]
    for copy in held_here:
        copy.start()
    barrier = pltpu.get_barrier_semaphore()
    greet = [gather_peer(1), gather_peer(2), gather_peer(3)]
    greet += [dest(r) for r in range(1, 8)]
    greet += [relay(r) for r in range(5, 8)]
    for v in greet:
        pl.semaphore_signal(barrier, inc=1, device_id=(y, v), device_id_type=MESH)
    for i in range(1, RING):
        pl.semaphore_signal(
            barrier, inc=1, device_id=((y + i) % RING, lax.axis_index("vert")), device_id_type=MESH
        )
    held_here[0].wait()
    held_here[1].wait()
    make_plan(cols, counts, z, x, core, plan_v)
    pl.semaphore_wait(barrier, len(greet) + RING - 1)

    def ask(row):
        return pltpu.make_async_remote_copy(
            src_ref=plan_v.at[row],
            dst_ref=codes_v.at[row],
            send_sem=req_send.at[row],
            recv_sem=req_recv.at[row],
            device_id=(y, relay(row)),
            device_id_type=MESH,
        )

    for row in range(1, 8):
        ask(row).start()

    gathered = {1: ag1, 2: ag2, 3: ag3}
    lower, upper = pl.ds(0, 8), pl.ds(8, 8)

    def share(j, half):
        rows = upper if half else lower
        source = (ag3 if half else ag1) if j == 2 else feat_in
        there = gather_peer((1 if half else 3) if j == 2 else RING - j)
        return pltpu.make_async_remote_copy(
            src_ref=source.at[rows],
            dst_ref=gathered[j].at[rows],
            send_sem=ag_send.at[j - 1, half],
            recv_sem=ag_recv.at[j - 1, half],
            device_id=(y, there),
            device_id_type=MESH,
        )

    share(1, 0).start()
    share(3, 1).start()
    share(1, 1).start()
    share(3, 0).start()

    mine_down = pltpu.make_async_copy(plan_v, plan, own_sem)
    mine_down.start()

    mine_down.wait()
    for row in range(1, 8):
        ask(row).wait()
    down = pltpu.make_async_copy(codes_v.at[pl.ds(1, 7)], codes.at[pl.ds(1, 7)], loc_sem)
    down.start()
    down.wait()

    def send(row, j):
        return pltpu.make_async_remote_copy(
            src_ref=stage.at[row, j],
            dst_ref=recv.at[row, j],
            send_sem=tile_send.at[row, j],
            recv_sem=tile_recv.at[row, j],
            device_id=(y, dest(row)),
            device_id_type=MESH,
        )

    def pass_on(j):
        source = gathered[j] if j else feat

        @pl.loop(1, 8)
        def _(row):
            for r in range(RANKS):
                stage[row, j, r] = source[codes[row, 0, j * RANKS + r]]
            send(row, j).start()

        for r in range(RANKS):
            recv[0, j, r] = source[plan[0, 0, j * RANKS + r]]

    lane_head = lax.broadcasted_iota(jnp.int32, (1, TILE), 1) // HS
    masks = [(lane_head == g).astype(jnp.float32).astype(jnp.bfloat16) for g in range(4)]

    def attend3(row, j):
        rows3 = recv[row, j].reshape(RANKS * TILE, D)
        keys3 = dot(rows3, wkv_in[:, :D]).astype(jnp.bfloat16)
        values3 = dot(wt[1], rows3, NT).astype(jnp.bfloat16)
        for r in range(RANKS):
            attend(row, j, r, keys3[r * TILE : (r + 1) * TILE], values3[:, r * TILE : (r + 1) * TILE])

    def attend(row, j, r, keys, values):
        n = (row * RING + j) * RANKS + r
        b = plan[8 + row, 0, j * RANKS + r]

        for g in range(4):
            s = dot(keys * jnp.concatenate([masks[g], masks[g]], axis=1), wq[b])
            m = jnp.max(s, axis=0, keepdims=True)
            e = jnp.exp2(s - m)
            t = jnp.sum(e, axis=0, keepdims=True)
            e = e.astype(jnp.bfloat16)
            for half in range(2):
                lanes = slice(half * TILE, (half + 1) * TILE)
                h = half * 4 + g
                top[n, h : h + 1] = m[:, lanes]
                total[n, h : h + 1] = t[:, lanes]
                part[n, h * HS : (h + 1) * HS] = dot(values[h * HS : (h + 1) * HS], e[:, lanes])

    def turn_of(t):
        k = jnp.maximum(t - 8, 0)
        pair = (k % 6) // 2
        far = jnp.where(pair == 0, 1, jnp.where(pair == 1, 3, 2)) + RING * (k % 2)
        near = jnp.where((t < 3) | (t == 6), 0, RING)
        row = jnp.where(t < 8, near, far)
        order = jnp.where(t < 3, t, jnp.where(t < 6, t - 3, jnp.where(t < 8, 3, k // 6)))
        return row, jnp.where(order == 2, 3, jnp.where(order == 3, 2, order))

    def attend_span(first, last):
        @pl.loop(first, last)
        def _(t):
            row, j = turn_of(t)

            @pl.when(row != 0)
            def _():
                send(row, j).wait_recv()

            attend3(row, j)

    share(1, 0).wait_recv()
    share(2, 0).start()
    share(3, 1).wait_recv()
    share(2, 1).start()
    for copy in held_here[2:]:
        copy.wait()

    wt[0] = wq_in[...].astype(jnp.float32).T.astype(jnp.bfloat16)
    wt[1] = wkv_in[:, D:].astype(jnp.float32).T.astype(jnp.bfloat16)

    @pl.loop(0, BLOCKS)
    def _(b):
        q = (dot(wt[0], feat[b], NT) * SCALE).astype(jnp.bfloat16)
        wq[b, :TILE, :TILE] = q[:TILE]
        wq[b, :TILE, TILE:] = jnp.zeros((TILE, TILE), jnp.bfloat16)
        wq[b, TILE:, :TILE] = jnp.zeros((TILE, TILE), jnp.bfloat16)
        wq[b, TILE:, TILE:] = q[TILE:]

    share(1, 1).wait_recv()
    share(3, 0).wait_recv()
    pass_on(0)
    pass_on(1)
    pass_on(3)
    attend_span(0, 3)
    share(2, 0).wait_recv()
    share(2, 1).wait_recv()
    pass_on(2)

    wt[2] = wqkv[:, :D].astype(jnp.float32).T.astype(jnp.bfloat16)
    wt[3] = wqkv[:, 2 * D :].astype(jnp.float32).T.astype(jnp.bfloat16)
    snaps = pos.shape[0]
    n = snaps * 8
    to = lax.broadcasted_iota(jnp.int32, (n, n), 0)
    source = lax.broadcasted_iota(jnp.int32, (n, n), 1)
    turn_s[0] = ((to % snaps) * 8 + to // snaps == source).astype(jnp.float32).astype(jnp.bfloat16)
    turn_s[1] = ((source % snaps) * 8 + source // snaps == to).astype(jnp.float32).astype(jnp.bfloat16)

    attend_span(3, 32)

    def combine(s):
        for u in range(2):
            b = s * 2 + u
            slots, live, tops = [], [], []
            for k in range(KT):
                slot = plan[16, 0, b * KT + k]
                alive = slot >= 0
                slot = jnp.where(alive, slot, 0)
                slots.append(slot)
                live.append(jnp.where(alive, jnp.float32(0), jnp.float32(-jnp.inf)))
                tops.append(top[slot] + live[k])
            m = functools.reduce(jnp.maximum, tops)
            weights = [jnp.exp2(t - m) for t in tops]
            denominator = sum(weights[k] * total[slots[k]] for k in range(KT))
            weights = [w / denominator for w in weights]
            parts = []
            for h in range(HEADS):
                parts.append(
                    sum(
                        weights[k][h : h + 1] * part[slots[k], h * HS : (h + 1) * HS]
                        for k in range(KT)
                    )
                )
            attended = jnp.concatenate(parts, axis=0).T.astype(jnp.bfloat16)
            update = dot(attended, wso[...])
            hid[s, u * TILE : (u + 1) * TILE] = (feat[b].astype(jnp.float32) + update).astype(
                jnp.bfloat16
            )


    def spread(i, chunk, half):
        group = (y + i) % RING
        return pltpu.make_async_remote_copy(
            src_ref=hid.at[pl.ds(half * 4, 4), pl.ds(group * 64 + chunk * 16, 16)],
            dst_ref=arr.at[pl.ds(y * 8 + half * 4, 4), pl.ds(chunk * 16, 16)],
            send_sem=snap_send.at[half, chunk, i],
            recv_sem=snap_recv.at[half, chunk, i],
            device_id=(group, lax.axis_index("vert")),
            device_id_type=MESH,
        )

    pl.loop(0, 4)(combine)
    for chunk in range(2):
        for i in (2, 1, 3):
            spread(i, chunk, 0).start()
    pl.loop(4, 8)(combine)
    for chunk in range(4):
        for half in range(2):
            if half or chunk >= 2:
                for i in (2, 1, 3):
                    spread(i, chunk, half).start()
    arr[pl.ds(y * 8, 8)] = hid[:, pl.ds(y * 64, 64)]

    lane = lax.broadcasted_iota(jnp.int32, (1, 1, TILE), 2)
    key_snap = lax.broadcasted_iota(jnp.int32, (1, snaps, 1), 1)
    query_snap = lane % snaps
    own_lane = [lane // snaps == v for v in range(4)]
    positions = pos[...].astype(jnp.float32)[:, None, :]

    vertex_of = [lax.broadcasted_iota(jnp.int32, (TILE, TILE), axis) // snaps for axis in range(2)]
    same_vertex = (vertex_of[0] == vertex_of[1]).astype(jnp.float32).astype(jnp.bfloat16)

    def write(step):
        return pltpu.make_async_copy(held.at[step], out.at[:, pl.ds(step * 16, 16)], out_sem.at[step])

    @pl.loop(0, 4)
    def _(step):
        for i in range(1, RING):
            for half in range(2):
                spread(i, step, half).wait_recv()
        hidden = arr[:, pl.ds(step * 16, 16)].astype(jnp.float32)
        groups = []
        for g in range(2):
            mine = hidden[:, g * 8 : (g + 1) * 8]
            rows = (mine + positions).reshape(n, D).astype(jnp.bfloat16)
            groups.append(dot(turn_s[0], rows).astype(jnp.bfloat16))
        rows = jnp.concatenate(groups, axis=0)
        q2 = (dot(wt[2], rows, NT) * SCALE).astype(jnp.bfloat16)
        keys2 = dot(rows, wqkv[:, D : 2 * D]).astype(jnp.bfloat16)
        values2 = dot(wt[3], rows, NT).astype(jnp.bfloat16)
        for g in range(2):
            base = y * 64 + step * 16 + g * 8
            mine = hidden[:, g * 8 : (g + 1) * 8]
            q, keys, values = q2[:, g * n : (g + 1) * n], keys2[g * n : (g + 1) * n], values2[:, g * n : (g + 1) * n]
            sides = []
            for u in range(2):
                birth = jnp.zeros((1, 1, TILE), jnp.int32)
                for v in range(4):
                    birth = jnp.where(own_lane[v], births[base + u * 4 + v], birth)
                allowed = (query_snap == key_snap) | ((query_snap >= key_snap) & (key_snap >= birth))
                bias = jnp.where(allowed, jnp.float32(0), jnp.float32(-jnp.inf))
                mixed = []
                for half in range(2):
                    kh = keys[u * TILE : (u + 1) * TILE, half * TILE : (half + 1) * TILE]
                    qh = q[half * TILE : (half + 1) * TILE, u * TILE : (u + 1) * TILE]
                    s = dot(jnp.concatenate([kh * w for w in masks], axis=0), qh)
                    s = s.reshape(4, 4, snaps, TILE)
                    near = s[:, 0]
                    for v in range(1, 4):
                        near = jnp.where(own_lane[v], s[:, v], near)
                    near = near + bias
                    m = jnp.max(near, axis=1, keepdims=True)
                    e = jnp.exp2(near - m)
                    t = 1.0 / jnp.sum(e, axis=1, keepdims=True)
                    for h in range(4):
                        wide = jnp.concatenate([e[h].astype(jnp.bfloat16)] * 4, axis=0) * same_vertex
                        top = (half * 4 + h) * HS
                        o = dot(values[top : top + HS, u * TILE : (u + 1) * TILE], wide)
                        mixed.append((o * t[h]).astype(jnp.bfloat16))
                sides.append(jnp.concatenate(mixed, axis=0))
            mixed = dot(turn_s[1], jnp.concatenate(sides, axis=1), NT).astype(jnp.bfloat16)
            held[step, :, g * 8 : (g + 1) * 8] = mine + dot(mixed, wo[...]).reshape(snaps, 8, D)
        write(step).start()

    for chunk in range(4):
        write(chunk).wait()
        for i in range(1, RING):
            for half in range(2):
                spread(i, chunk, half).wait_send()
    for j, half in ((1, 0), (1, 1), (2, 0), (2, 1), (3, 0), (3, 1)):
        share(j, half).wait_send()
    for j in range(RING):

        @pl.loop(1, 8)
        def _(row):
            send(row, j).wait_send()


def local(features, tile_cols, counts, births, wq, wkv, wso, pos, wqkv, wo):
    snaps, rows, width = features.shape
    hbm = pl.BlockSpec(memory_space=pltpu.HBM)
    dma = pltpu.SemaphoreType.DMA
    half = jnp.bfloat16
    count = rows // RING
    result = pl.pallas_call(
        graph_kernel,
        out_shape=jax.ShapeDtypeStruct((RING * snaps, count, width), jnp.float32),
        in_specs=[hbm] * 10,
        out_specs=pl.BlockSpec(memory_space=pl.ANY),
        scratch_shapes=[
            pltpu.SMEM((rows // TILE, KT, snaps), jnp.int32),
            pltpu.SMEM((rows // TILE, snaps), jnp.int32),
            pltpu.SMEM(births.shape, jnp.int32),
            pltpu.VMEM((BLOCKS, TILE, width), half),
            pltpu.VMEM(wq.shape, half),
            pltpu.VMEM(wkv.shape, half),
            pltpu.VMEM(wso.shape, half),
            pltpu.VMEM(pos.shape, half),
            pltpu.VMEM(wqkv.shape, half),
            pltpu.VMEM(wo.shape, half),
            pltpu.VMEM((17, 1, TILE), jnp.int32),
            pltpu.SMEM((17, 1, TILE), jnp.int32),
            pltpu.VMEM((8, 1, TILE), jnp.int32),
            pltpu.SMEM((8, 1, TILE), jnp.int32),
            pltpu.VMEM((BLOCKS, TILE, width), half),
            pltpu.VMEM((BLOCKS, TILE, width), half),
            pltpu.VMEM((BLOCKS, TILE, width), half),
            pltpu.VMEM((8, RING, RANKS, TILE, width), half),
            pltpu.VMEM((8, RING, RANKS, TILE, width), half),
            pltpu.VMEM((BLOCKS, width, width), half),
            pltpu.VMEM((4, width, width), half),
            pltpu.VMEM((2, RING * snaps * 8, RING * snaps * 8), half),
            pltpu.VMEM((SLOTS, width, TILE), jnp.float32),
            pltpu.VMEM((SLOTS, HEADS, TILE), jnp.float32),
            pltpu.VMEM((SLOTS, HEADS, TILE), jnp.float32),
            pltpu.VMEM((snaps, rows, width), half),
            pltpu.VMEM((RING * snaps, count, width), half),
            pltpu.VMEM((RING, RING * snaps, 16, width), jnp.float32),
            dma((8,)), dma((8,)), dma, dma((3, 2)), dma((3, 2)),
            dma((8, RING)), dma((8, RING)), dma((2, 4, RING)), dma((2, 4, RING)), dma, dma((4,)), dma((10,)),
        ],
        compiler_params=pltpu.CompilerParams(
            collective_id=0, has_side_effects=True, vmem_limit_bytes=58 * 2**20
        ),
        name="graph",
    )(tile_cols.transpose(1, 2, 0), counts.T, births, features.reshape(BLOCKS, TILE, width), wq, wkv, wso, pos, wqkv, wo)
    return result[:, None, None]


def solution(mesh):
    placed = (
        P("snap", "vert", None), P("snap", "vert", None), P("snap", "vert"), P("vert"),
        P(), P(), P(), P(), P(), P(),
    )
    return jax.shard_map(
        local,
        mesh=mesh,
        in_specs=placed,
        out_specs=P(None, "vert", "snap", None, None),
        check_vma=False,
    )
```
